128 devices in a mesh: row: 32 (over y, z, core), col: 4 (over x).
Axes of the slice: x: 4, y: 4, z: 4, core: 2. Of those that a mesh axis runs over, the one named last changes fastest.
Arguments:
- factor: float32 [4, 4096, 52, 512], P(None, 'row', None, 'col'), may hold values from -0.0390625 to 0.0390625
- earlier: float32 [20, 512, 256], P(None, 'col'), may hold values from -6 to 6
- rhs: float32 [4, 4096, 256], P(None, 'row'), may hold values from -6 to 6
- inverse: float32 [4, 4096, 4096], P(None, 'row'), may hold values from -1.4 to 1.4, as said below
Outputs:
- solution: float32 [4, 4096, 256], P(None, 'row')
The draws below stay inside these ranges and needn't reach their ends.
Inputs may be any that keep to these rules, and one draw needn't show every extreme that they name: Each [4096, 4096] block of inverse is lower triangular, with diagonal entries from 0.6 to 1.4.
All inputs are finite; a program needn't handle non-finite values.
Results may differ from the reference program's by a relative error of at most 0.0001.
Values sent between devices are 32-bit elements; how exact they have to be, the bound alone decides.
A program may use at most 128 MiB of HBM per device.

```python
import jax
import jax.numpy as jnp
from jax import lax

NB = 128
RHS = 256
STEPS = 4
P_SIZE = 10240
BS = 4096
ORDER = 26624
QC = 52
QP = 20
N_COL = 4


def draw_inverse(key, part):
    key = jax.random.fold_in(key, 7)
    diag_key, lower_key = jax.random.split(key)
    position = jnp.arange(BS)[None, :, None]
    column = jnp.arange(BS)[None, None, :]
    reach = (3.0 / BS) ** 0.5
    diag_value = jax.random.uniform(diag_key, (STEPS, BS, BS), jnp.float32, 0.6, 1.4)
    lower_value = jax.random.uniform(lower_key, (STEPS, BS, BS), jnp.float32, -reach, reach)
    return jnp.where(column < position, lower_value, 0.0) + jnp.where(column == position, diag_value, 0.0)


def block_scale(own_key, shape, pieces, smallest, high):
    def one(dim, shards_of):
        steps = jax.random.uniform(jax.random.fold_in(jax.random.fold_in(own_key, 6), dim), (shards_of,), jnp.float32, smallest / len(pieces), high / len(pieces))
        return jnp.repeat(jnp.exp(steps), shape[dim] // shards_of).reshape((-1,) + (1,) * (len(shape) - dim - 1))

    factor_of = one(*pieces[0])
    for cut in pieces[1:]:
        factor_of = factor_of * one(*cut)
    return factor_of


def gaussian(stream_key, shape, width, most, shards=(), kind=jnp.bfloat16):
    drawn = jax.random.normal(stream_key, shape, jnp.float32) * width
    if len(shards) > 0:
        drawn = block_scale(stream_key, shape, shards, -0.22, 0.18) * drawn
    return jnp.clip(drawn, min=-most, max=most).astype(kind)


def setup_inputs(seed: int = 0) -> dict:
    key_list = jax.random.split(jax.random.key(seed), 5)
    return {
        "factor": gaussian(key_list[0], (STEPS, BS, QC, N_COL * NB), ORDER ** -0.5, 0.0390625, ((1, 32), (3, 4)), jnp.float32),
        "earlier": gaussian(key_list[1], (QP, N_COL * NB, RHS), 1.0, 6.0, ((1, 4),), jnp.float32),
        "rhs": gaussian(key_list[2], (STEPS, BS, RHS), 1.0, 6.0, ((1, 32),), jnp.float32),
        "inverse": draw_inverse(jax.random.fold_in(key_list[4], 71), 0),
    }


def reference(factor, earlier, rhs, inverse):
    full_rows = factor.reshape(STEPS * BS, ORDER)
    known_rows = earlier.reshape(P_SIZE, RHS)
    rhs_rows = rhs.reshape(STEPS * BS, RHS)
    base_rhs = rhs_rows - jnp.dot(full_rows[:, :P_SIZE], known_rows, precision=lax.Precision.HIGHEST, preferred_element_type=jnp.float32)
    solved_blocks = []
    for step in range(STEPS):
        partial_rhs = base_rhs[step * BS:(step + 1) * BS]
        if step > 0:
            left_part = full_rows[step * BS:(step + 1) * BS, P_SIZE:P_SIZE + step * BS]
            partial_rhs = partial_rhs - jnp.dot(left_part, jnp.concatenate(solved_blocks, 0), precision=lax.Precision.HIGHEST, preferred_element_type=jnp.float32)
        solved_blocks.append(jnp.dot(inverse[step], partial_rhs, precision=lax.Precision.HIGHEST, preferred_element_type=jnp.float32))
    return jnp.stack(solved_blocks, 0)
```

```python
import functools

import jax
import jax.numpy as jnp
from jax import lax
from jax.experimental import pallas as pl
from jax.experimental.pallas import tpu as pltpu
from jax.sharding import PartitionSpec as P

F32 = jnp.float32
BF16 = jnp.bfloat16
MESH = pl.DeviceIdType.MESH
STEPS = 4
KNOWN = 20
GROUPS = 8
CHAINS = 2
T = 32
PAIRS = [(1, 0), (2, 0), (2, 1), (3, 0), (3, 1), (3, 2)]
SLOT = {pair: index for index, pair in enumerate(PAIRS)}


def halves(value):
    high = value.astype(BF16)
    return high, (value - high.astype(F32)).astype(BF16)


def dot(left, right):
    return lax.dot_general(left, right, (((1,), (0,)), ((), ())), preferred_element_type=F32)


def kernel(
    factor, earlier, rhs, inverse, out,
    y_raw, y_parts, f_raw, f_parts, u_raw, u_parts, i_raw, i_parts, b_raw, b_turn,
    known, known_in, start, res, sol, upd_in, part_in, part, upd, later, done, turned, a_res, a_sol,
    ld, sib_s, sib_r, kn_s, kn_r, g1_s, g1_r, pt_s, pt_r, g2_s, g2_r, ot_s, ot_r, up_s, up_r, wr,
):
    row = lax.axis_index("row")
    x = lax.axis_index("col")
    y, z, j = row // 8, (row // 2) % 4, row % 2
    m = row // 2

    def at(x_, y_, z_, j_):
        return ((y_ * 4 + z_) * 2 + j_, x_)

    sibling = at(x, y, z, 1 - j)
    spread = x // 2
    own_zone = (z % 2) == (x // 2)
    g_here = jnp.where(own_zone, 0, 1)
    z_row = jnp.where(own_zone, z, (z + 3) % 4)
    q_here = 2 * g_here + j
    sol_slot = g_here * 8 + y * 2 + z_row // 2
    self_part = (z % 2 == 0) & (x < 2) & (j == x)
    self_out = own_zone & (x % 2 == j)
    self_upd = (x % 2) == j

    def send(src, dst, ss, rs, device):
        pltpu.make_async_remote_copy(
            src_ref=src, dst_ref=dst, send_sem=ss, recv_sem=rs, device_id=device, device_id_type=MESH
        ).start()

    def wait_recv(ref, sem):
        pltpu.make_async_remote_copy(
            src_ref=ref, dst_ref=ref, send_sem=sem, recv_sem=sem, device_id=sibling, device_id_type=MESH
        ).wait_recv()

    def wait_send(ref, sem):
        pltpu.make_async_remote_copy(
            src_ref=ref, dst_ref=ref, send_sem=sem, recv_sem=sem, device_id=sibling, device_id_type=MESH
        ).wait_send()

    def wait_local(ref, sem):
        pltpu.make_async_copy(ref, ref, sem).wait()

    def loop(lo, hi, body):
        lax.fori_loop(lo, hi, lambda index, carry: (body(index), carry)[1], 0)

    def load_known(step):
        def one(group):
            pltpu.make_async_copy(factor.at[step, :, group, :], f_raw.at[step, group], ld.at[2 + step]).start()

        loop(0, KNOWN, one)

    def load_inverse(step):
        def one(tile):
            lanes = pl.ds(pl.multiple_of((2 * tile + j) * 128, 128), 128)
            pltpu.make_async_copy(inverse.at[step, :, lanes], i_raw.at[step, j, tile], ld.at[6 + step]).start()

        loop(0, 16, one)

    def share_inverse(step):
        def one(tile):
            lanes = pl.ds(pl.multiple_of((2 * tile + 1 - j) * 128, 128), 128)
            send(inverse.at[step, :, lanes], i_raw.at[step, j, tile], sib_s.at[step], sib_r.at[step], sibling)

        loop(0, 16, one)

    def load_update(pair):
        later_step, step = pair
        slot = SLOT[pair]

        def one(group):
            pltpu.make_async_copy(
                factor.at[later_step, :, KNOWN + step * GROUPS + group, :], u_raw.at[slot, j, group], ld.at[10 + slot]
            ).start()

        loop(0, GROUPS, one)

    def share_update(pair):
        slot = SLOT[pair]
        wait_local(u_raw.at[slot, j], ld.at[10 + slot])
        send(u_raw.at[slot, j], u_raw.at[slot, j], sib_s.at[4 + slot], sib_r.at[4 + slot], sibling)

    def prepare_inverse(step):
        wait_local(i_raw.at[step, j], ld.at[6 + step])
        wait_recv(i_raw.at[step, 1 - j], sib_r.at[step])

        def one(tile):
            rows = pl.ds(pl.multiple_of(tile * 128, 128), 128)
            for t in range(2):
                high, low = halves(i_raw[step, t, tile])
                i_parts[step, rows, t * 256 : t * 256 + 128] = high.T
                i_parts[step, rows, t * 256 + 128 : t * 256 + 256] = low.T

        loop(0, 16, one)

    def prepare_update(pair):
        slot = SLOT[pair]
        wait_recv(u_raw.at[slot, 1 - j], sib_r.at[4 + slot])

        def one(group):
            rows = pl.ds(pl.multiple_of(group * 128, 128), 128)
            for t in range(2):
                high, low = halves(u_raw[slot, t, group])
                u_parts[slot, rows, t * 256 : t * 256 + 128] = high.T
                u_parts[slot, rows, t * 256 + 128 : t * 256 + 256] = low.T

        loop(0, GROUPS, one)

    def known_terms(step):
        wait_local(f_raw.at[step], ld.at[2 + step])

        def one(group):
            lanes = pl.ds(pl.multiple_of(group * 128, 128), 128)
            high, low = halves(f_raw[step, group])
            f_parts[0:128, lanes] = high
            f_parts[128:256, lanes] = low

        loop(0, KNOWN, one)
        both = dot(f_parts[...], y_parts[...])
        total = both[0:128, 0:256] + (both[0:128, 256:512] + both[128:256, 0:256] + both[128:256, 256:512])
        known[step] = -(total.T)
        b_turn[...] = b_raw[step].T
        mine = pl.ds(pl.multiple_of(x * 64, 64), 64)
        known_in[step, x] = b_turn[mine] + known[step, mine]

    def send_known(step):
        for hop in (2, 1, 3):
            q = (x + hop) % 4
            rows = pl.ds(pl.multiple_of(q * 64, 64), 64)
            send(known.at[step, rows], known_in.at[step, x], kn_s.at[step], kn_r.at[step], at(q, y, z, j))

    def collect_known(step):
        wait_recv(known_in.at[step, pl.ds(0, 3)], kn_r.at[step])
        total = known_in[step, 0] + known_in[step, 1] + known_in[step, 2] + known_in[step, 3]
        for h in range(CHAINS):
            start[step, h] = total[h * T : (h + 1) * T]

    def send_residual(step, h):
        if step == 0:
            res[step, h, m] = start[step, h]
        else:

            @pl.when(self_upd)
            def _():
                wait_recv(upd_in.at[step - 1, h, pl.ds(0, 3)], up_r.at[step - 1, h])

            @pl.when(jnp.logical_not(self_upd))
            def _():
                wait_recv(upd_in.at[step - 1, h], up_r.at[step - 1, h])

            res[step, h, m] = start[step, h] + (
                upd_in[step - 1, h, 0] + upd_in[step - 1, h, 1] + upd_in[step - 1, h, 2] + upd_in[step - 1, h, 3]
            )

        def one(other):
            send(
                res.at[step, h, m], res.at[step, h, m], g1_s.at[step, h, other], g1_r.at[step, h, m],
                at(x, other // 4, other % 4, j),
            )

        loop(m + 1, 16, one)

    def drain_residual(step, h):
        def one(other):
            wait_send(res.at[step, h, m], g1_s.at[step, h, other])

        loop(m + 1, 16, one)

    def solve(step, h):
        def place(tile):
            lanes = pl.ds(pl.multiple_of(tile * 128, 128), 128)
            high, low = halves(res[step, h, tile])
            a_res[h, 0:T, lanes] = high
            a_res[h, T : 2 * T, lanes] = low

        def arrived(tile):
            wait_recv(res.at[step, h, tile], g1_r.at[step, h, tile])
            place(tile)

        place(m)
        loop(0, m, arrived)
        both = dot(a_res[h], i_parts[step])
        for t in range(2):
            o = t * 256
            part[step, h, t] = both[0:T, o : o + 128] + (
                both[0:T, o + 128 : o + 256] + both[T : 2 * T, o : o + 128] + both[T : 2 * T, o + 128 : o + 256]
            )

        def to(t):
            send(
                part.at[step, h, t], part_in.at[step, h, j], pt_s.at[step, h, t], pt_r.at[step, h, j],
                at((z % 2) * 2 + t, y, (z + spread) % 4, x % 2),
            )

        for t in range(2):
            here = self_part & (x == t)

            @pl.when(here)
            def _():
                part_in[step, h, j] = part[step, h, t]

            @pl.when(jnp.logical_not(here))
            def _():
                to(t)

    def drain_part(step, h):
        for t in range(2):

            @pl.when(jnp.logical_not(self_part & (x == t)))
            def _():
                wait_send(part.at[step, h, t], pt_s.at[step, h, t])

    def send_solution(step, h):
        for k in range(2):

            @pl.when(jnp.logical_not(self_part & (j == k)))
            def _():
                wait_recv(part_in.at[step, h, k], pt_r.at[step, h, k])

        sol[step, h, sol_slot] = part_in[step, h, 0] + part_in[step, h, 1]
        mine = sol.at[step, h, sol_slot]
        if step + 1 < STEPS:

            def one(index):
                other = (9 + index) % 15 + 1
                send(
                    mine, mine, g2_s.at[step, h], g2_r.at[step, h],
                    at(x, (y + other // 4) % 4, (z + other % 4) % 4, j),
                )

            loop(0, 15, one)
        rows = pl.ds(pl.multiple_of(q_here * 64 + h * T, T), T)
        for hop in (2, 1, 3):
            send(mine, done.at[step, rows], ot_s.at[step, h], ot_r.at[step], at((x + hop) % 4, y, z_row, x % 2))

        @pl.when(self_out)
        def _():
            done[step, rows] = sol[step, h, sol_slot]

        @pl.when(jnp.logical_not(self_out))
        def _():
            send(mine, done.at[step, rows], ot_s.at[step, h], ot_r.at[step], at(x, y, z_row, x % 2))

    def drain_solution(step, h):
        if step + 1 < STEPS:
            wait_send(sol.at[step, h, pl.ds(0, 15)], g2_s.at[step, h])

        @pl.when(self_out)
        def _():
            wait_send(sol.at[step, h, pl.ds(0, 3)], ot_s.at[step, h])

        @pl.when(jnp.logical_not(self_out))
        def _():
            wait_send(sol.at[step, h, pl.ds(0, 4)], ot_s.at[step, h])

    def gather_solution(step, h):
        wait_recv(sol.at[step, h, pl.ds(0, 15)], g2_r.at[step, h])
        for g in range(2):
            for b in range(GROUPS):
                high, low = halves(sol[step, h, g * 8 + b])
                a_sol[h, g * T : (g + 1) * T, b * 128 : (b + 1) * 128] = high
                a_sol[h, 2 * T + g * T : 2 * T + (g + 1) * T, b * 128 : (b + 1) * 128] = low

    def update(step, later_step, h):
        both = dot(a_sol[h], u_parts[SLOT[later_step, step]])
        for t in range(2):
            o = t * 256
            total = both[0 : 2 * T, o : o + 128] + (
                both[0 : 2 * T, o + 128 : o + 256]
                + both[2 * T : 4 * T, o : o + 128]
                + both[2 * T : 4 * T, o + 128 : o + 256]
            )
            if step > 0:
                total = total + later[later_step - 2, h, t]
            if later_step > step + 1:
                later[later_step - 2, h, t] = total
            else:
                for g in range(2):
                    upd[step, h, t, g] = -total[g * T : (g + 1) * T]
        if later_step > step + 1:
            return
        for t in range(2):
            for g in range(2):
                here = (x == 2 * g + j) & (j == t)

                @pl.when(here)
                def _():
                    upd_in[step, h, x] = upd[step, h, t, g]

                @pl.when(jnp.logical_not(here))
                def _():
                    send(
                        upd.at[step, h, t, g], upd_in.at[step, h, x], up_s.at[step, h], up_r.at[step, h],
                        at(2 * g + j, y, z, t),
                    )

    def drain_update(step, h):
        @pl.when(self_upd)
        def _():
            wait_send(upd_in.at[step, h, pl.ds(0, 3)], up_s.at[step, h])

        @pl.when(jnp.logical_not(self_upd))
        def _():
            wait_send(upd_in.at[step, h], up_s.at[step, h])

    def write(step):
        @pl.when(self_out)
        def _():
            wait_recv(done.at[step, pl.ds(0, 6 * T)], ot_r.at[step])

        @pl.when(jnp.logical_not(self_out))
        def _():
            wait_recv(done.at[step], ot_r.at[step])

        turned[step] = done[step].T
        pltpu.make_async_copy(turned.at[step], out.at[step], wr.at[step]).start()

    barrier = pltpu.get_barrier_semaphore()

    def greet(device):
        pl.semaphore_signal(barrier, inc=1, device_id=device, device_id_type=MESH)

    pltpu.make_async_copy(earlier, y_raw, ld.at[0]).start()
    load_known(0)
    pltpu.make_async_copy(rhs, b_raw, ld.at[1]).start()
    load_inverse(0)

    def greet_plane(other):
        greet(at(x, (y + other // 4) % 4, (z + other % 4) % 4, j))

    loop(1, 16, greet_plane)
    for hop in range(4):
        for core in range(2):
            if (hop, core) != (0, 0):
                greet(at((x + hop) % 4, y, z, (j + core) % 2))
            greet(at((x + hop) % 4, y, (z + 1) % 4, (j + core) % 2))
            greet(at((x + hop) % 4, y, (z + 3) % 4, (j + core) % 2))
    a_res[...] = jnp.zeros_like(a_res)
    wait_local(y_raw, ld.at[0])

    def split_earlier(group):
        rows = pl.ds(pl.multiple_of(group * 128, 128), 128)
        high, low = halves(y_raw[group])
        y_parts[rows, 0:256] = high
        y_parts[rows, 256:512] = low

    loop(0, KNOWN, split_earlier)
    wait_local(b_raw, ld.at[1])
    known_terms(0)
    pl.semaphore_wait(barrier, 15 + 7 + 16)
    send_known(0)
    share_inverse(0)
    load_update(PAIRS[0])
    load_known(1)
    share_update(PAIRS[0])
    load_known(2)
    load_known(3)
    collect_known(0)
    for h in range(CHAINS):
        send_residual(0, h)
    prepare_inverse(0)
    for step in range(1, STEPS):
        load_inverse(step)
    for pair in PAIRS[1:]:
        load_update(pair)

    for step in range(STEPS):
        for h in range(CHAINS):
            solve(step, h)
        if step == 0:
            prepare_update(PAIRS[0])
            known_terms(1)
            send_known(1)
        elif step + 1 < STEPS:
            for h in range(CHAINS):
                drain_residual(step - 1, h)
                drain_solution(step - 1, h)
                drain_part(step - 1, h)
        for h in range(CHAINS):
            send_solution(step, h)
        if step + 1 == STEPS:
            break
        if step == 0:
            share_inverse(1)
            for pair in PAIRS[1:]:
                share_update(pair)
            known_terms(2)
            send_known(2)
            known_terms(3)
            send_known(3)
            collect_known(1)
            prepare_update((2, 0))
            prepare_update((3, 0))
        elif step == 1:
            share_inverse(3)
            prepare_inverse(2)
        for h in range(CHAINS):
            gather_solution(step, h)
            update(step, step + 1, h)
        for later_step in range(step + 2, STEPS):
            for h in range(CHAINS):
                update(step, later_step, h)
        if step == 0:
            share_inverse(2)
            collect_known(2)
            collect_known(3)
        for h in range(CHAINS):
            send_residual(step + 1, h)
        if step == 0:
            prepare_inverse(1)
            prepare_update((2, 1))
            prepare_update((3, 1))
        elif step == 1:
            prepare_inverse(3)
            prepare_update((3, 2))
        write(step)
        for h in range(CHAINS):
            drain_update(step, h)

    for step in range(STEPS):
        wait_send(known.at[step, pl.ds(0, 192)], kn_s.at[step])
        wait_send(i_raw.at[step, j], sib_s.at[step])
    for slot in range(len(PAIRS)):
        wait_send(u_raw.at[slot, j], sib_s.at[4 + slot])
    for step in range(STEPS - 2, STEPS):
        for h in range(CHAINS):
            drain_residual(step, h)
            drain_part(step, h)
            drain_solution(step, h)
    write(STEPS - 1)
    for step in range(STEPS):
        wait_local(turned.at[step], wr.at[step])


def per_device(factor, earlier, rhs, inverse):
    dma = pltpu.SemaphoreType.DMA
    vmem = pltpu.VMEM
    updates = len(PAIRS)
    return pl.pallas_call(
        kernel,
        out_shape=jax.ShapeDtypeStruct(rhs.shape, F32),
        in_specs=[pl.BlockSpec(memory_space=pl.ANY)] * 4,
        out_specs=pl.BlockSpec(memory_space=pl.ANY),
        scratch_shapes=[
            vmem((KNOWN, 128, 256), F32),
            vmem((KNOWN * 128, 512), BF16),
            vmem((STEPS, KNOWN, 128, 128), F32),
            vmem((256, KNOWN * 128), BF16),
            vmem((updates, 2, GROUPS, 128, 128), F32),
            vmem((updates, GROUPS * 128, 512), BF16),
            vmem((STEPS, 2, 16, 128, 128), F32),
            vmem((STEPS, 2048, 512), BF16),
            vmem((STEPS, 128, 256), F32),
            vmem((256, 128), F32),
            vmem((STEPS, 256, 128), F32),
            vmem((STEPS, 4, 64, 128), F32),
            vmem((STEPS, CHAINS, T, 128), F32),
            vmem((STEPS, CHAINS, 16, T, 128), F32),
            vmem((STEPS, CHAINS, 16, T, 128), F32),
            vmem((STEPS - 1, CHAINS, 4, T, 128), F32),
            vmem((STEPS, CHAINS, 2, T, 128), F32),
            vmem((STEPS, CHAINS, 2, T, 128), F32),
            vmem((STEPS - 1, CHAINS, 2, 2, T, 128), F32),
            vmem((2, CHAINS, 2, 2 * T, 128), F32),
            vmem((STEPS, 256, 128), F32),
            vmem((STEPS, 128, 256), F32),
            vmem((CHAINS, 2 * T, 2048), BF16),
            vmem((CHAINS, 4 * T, 1024), BF16),
            dma((16,)),
            dma((10,)),
            dma((10,)),
            dma((STEPS,)),
            dma((STEPS,)),
            dma((STEPS, CHAINS, 16)),
            dma((STEPS, CHAINS, 16)),
            dma((STEPS, CHAINS, 2)),
            dma((STEPS, CHAINS, 2)),
            dma((STEPS, CHAINS)),
            dma((STEPS, CHAINS)),
            dma((STEPS, CHAINS)),
            dma((STEPS,)),
            dma((STEPS, CHAINS)),
            dma((STEPS, CHAINS)),
            dma((STEPS,)),
        ],
        compiler_params=pltpu.CompilerParams(
            collective_id=0, has_side_effects=True, vmem_limit_bytes=60 * 1024 * 1024
        ),
        cost_estimate=pl.CostEstimate(flops=6_000_000_000, bytes_accessed=20_000_000, transcendentals=0),
        name="substitution",
    )(factor, earlier, rhs, inverse)


def solution(mesh):
    return jax.shard_map(
        per_device,
        mesh=mesh,
        in_specs=(
            P(None, "row", None, "col"),
            P(None, "col", None),
            P(None, "row", None),
            P(None, "row", None),
        ),
        out_specs=P(None, "row", None),
        check_vma=False,
    )
```

```python
import functools

import jax
import jax.numpy as jnp
from jax import lax
from jax.experimental import pallas as pl
from jax.experimental.pallas import tpu as pltpu
from jax.sharding import PartitionSpec as P

F32 = jnp.float32
BF16 = jnp.bfloat16
MESH = pl.DeviceIdType.MESH
STEPS = 4
KNOWN = 20
GROUPS = 8
CHAINS = 2
T = 32
PAIRS = [(1, 0), (2, 0), (2, 1), (3, 0), (3, 1), (3, 2)]
SLOT = {pair: index for index, pair in enumerate(PAIRS)}


def halves(value):
    high = value.astype(BF16)
    return high, (value - high.astype(F32)).astype(BF16)


def dot(left, right):
    return lax.dot_general(left, right, (((1,), (0,)), ((), ())), preferred_element_type=F32)


def kernel(
    factor, earlier, rhs, inverse, out,
    y_raw, y_parts, f_raw, f_parts, u_raw, u_parts, i_raw, i_parts, b_raw, b_turn,
    known, known_in, start, res, sol, upd_in, part_in, part, upd, later, done, turned, a_res, a_sol,
    ld, sib_s, sib_r, kn_s, kn_r, g1_s, g1_r, pt_s, pt_r, g2_s, g2_r, ot_s, ot_r, up_s, up_r, wr,
):
    row = lax.axis_index("row")
    x = lax.axis_index("col")
    y, z, j = row // 8, (row // 2) % 4, row % 2
    m = row // 2

    def at(x_, y_, z_, j_):
        return ((y_ * 4 + z_) * 2 + j_, x_)

    sibling = at(x, y, z, 1 - j)
    spread = x // 2
    own_zone = (z % 2) == (x // 2)
    g_here = jnp.where(own_zone, 0, 1)
    z_row = jnp.where(own_zone, z, (z + 3) % 4)
    q_here = 2 * g_here + j
    sol_slot = g_here * 8 + y * 2 + z_row // 2
    self_part = (z % 2 == 0) & (x < 2) & (j == x)
    self_out = own_zone & (x % 2 == j)
    self_upd = (x % 2) == j

    def send(src, dst, ss, rs, device):
        pltpu.make_async_remote_copy(
            src_ref=src, dst_ref=dst, send_sem=ss, recv_sem=rs, device_id=device, device_id_type=MESH
        ).start()

    def wait_recv(ref, sem):
        pltpu.make_async_remote_copy(
            src_ref=ref, dst_ref=ref, send_sem=sem, recv_sem=sem, device_id=sibling, device_id_type=MESH
        ).wait_recv()

    def wait_send(ref, sem):
        pltpu.make_async_remote_copy(
            src_ref=ref, dst_ref=ref, send_sem=sem, recv_sem=sem, device_id=sibling, device_id_type=MESH
        ).wait_send()

    def wait_local(ref, sem):
        pltpu.make_async_copy(ref, ref, sem).wait()

    def loop(lo, hi, body):
        lax.fori_loop(lo, hi, lambda index, carry: (body(index), carry)[1], 0)

    def load_known(step):
        pltpu.make_async_copy(factor.at[step, pl.ds(0, KNOWN)], f_raw.at[step], ld.at[2 + step]).start()

    def load_inverse(step):
        def one(tile):
            lanes = pl.ds(pl.multiple_of((2 * tile + j) * 128, 128), 128)
            pltpu.make_async_copy(inverse.at[step, :, lanes], i_raw.at[step, j, tile], ld.at[6 + step]).start()

        loop(0, 16, one)

    def share_inverse(step):
        def one(tile):
            lanes = pl.ds(pl.multiple_of((2 * tile + 1 - j) * 128, 128), 128)
            send(inverse.at[step, :, lanes], i_raw.at[step, j, tile], sib_s.at[step], sib_r.at[step], sibling)

        loop(0, 16, one)

    def load_update(pair):
        later_step, step = pair
        slot = SLOT[pair]
        groups = pl.ds(KNOWN + step * GROUPS, GROUPS)
        pltpu.make_async_copy(factor.at[later_step, groups], u_raw.at[slot, j], ld.at[10 + slot]).start()

    def share_update(pair):
        slot = SLOT[pair]
        wait_local(u_raw.at[slot, j], ld.at[10 + slot])
        send(u_raw.at[slot, j], u_raw.at[slot, j], sib_s.at[4 + slot], sib_r.at[4 + slot], sibling)

    def prepare_inverse(step):
        wait_local(i_raw.at[step, j], ld.at[6 + step])
        wait_recv(i_raw.at[step, 1 - j], sib_r.at[step])

        def one(tile):
            rows = pl.ds(pl.multiple_of(tile * 128, 128), 128)
            for t in range(2):
                high, low = halves(i_raw[step, t, tile])
                i_parts[step, rows, t * 256 : t * 256 + 128] = high.T
                i_parts[step, rows, t * 256 + 128 : t * 256 + 256] = low.T

        loop(0, 16, one)

    def prepare_update(pair):
        slot = SLOT[pair]
        wait_recv(u_raw.at[slot, 1 - j], sib_r.at[4 + slot])

        def one(group):
            rows = pl.ds(pl.multiple_of(group * 128, 128), 128)
            for t in range(2):
                high, low = halves(u_raw[slot, t, group])
                u_parts[slot, rows, t * 256 : t * 256 + 128] = high.T
                u_parts[slot, rows, t * 256 + 128 : t * 256 + 256] = low.T

        loop(0, GROUPS, one)

    def known_terms(step):
        wait_local(f_raw.at[step], ld.at[2 + step])

        def one(group):
            lanes = pl.ds(pl.multiple_of(group * 128, 128), 128)
            high, low = halves(f_raw[step, group])
            f_parts[0:128, lanes] = high
            f_parts[128:256, lanes] = low

        loop(0, KNOWN, one)
        both = dot(f_parts[...], y_parts[...])
        total = both[0:128, 0:256] + (both[0:128, 256:512] + both[128:256, 0:256] + both[128:256, 256:512])
        known[step] = -(total.T)
        b_turn[...] = b_raw[step].T
        mine = pl.ds(pl.multiple_of(x * 64, 64), 64)
        known_in[step, x] = b_turn[mine] + known[step, mine]

    def send_known(step):
        for hop in (2, 1, 3):
            q = (x + hop) % 4
            rows = pl.ds(pl.multiple_of(q * 64, 64), 64)
            send(known.at[step, rows], known_in.at[step, x], kn_s.at[step], kn_r.at[step], at(q, y, z, j))

    def collect_known(step):
        wait_recv(known_in.at[step, pl.ds(0, 3)], kn_r.at[step])
        total = known_in[step, 0] + known_in[step, 1] + known_in[step, 2] + known_in[step, 3]
        for h in range(CHAINS):
            start[step, h] = total[h * T : (h + 1) * T]

    def send_residual(step, h):
        if step == 0:
            res[step, h, m] = start[step, h]
        else:

            @pl.when(self_upd)
            def _():
                wait_recv(upd_in.at[step - 1, h, pl.ds(0, 3)], up_r.at[step - 1, h])

            @pl.when(jnp.logical_not(self_upd))
            def _():
                wait_recv(upd_in.at[step - 1, h], up_r.at[step - 1, h])

            res[step, h, m] = start[step, h] + (
                upd_in[step - 1, h, 0] + upd_in[step - 1, h, 1] + upd_in[step - 1, h, 2] + upd_in[step - 1, h, 3]
            )

        def one(other):
            send(
                res.at[step, h, m], res.at[step, h, m], g1_s.at[step, h, other], g1_r.at[step, h, m],
                at(x, other // 4, other % 4, j),
            )

        loop(m + 1, 16, one)

    def drain_residual(step, h):
        def one(other):
            wait_send(res.at[step, h, m], g1_s.at[step, h, other])

        loop(m + 1, 16, one)

    def solve(step, h):
        def place(tile):
            lanes = pl.ds(pl.multiple_of(tile * 128, 128), 128)
            high, low = halves(res[step, h, tile])
            a_res[h, 0:T, lanes] = high
            a_res[h, T : 2 * T, lanes] = low

        def arrived(tile):
            wait_recv(res.at[step, h, tile], g1_r.at[step, h, tile])
            place(tile)

        place(m)
        loop(0, m, arrived)
        both = dot(a_res[h], i_parts[step])
        for t in range(2):
            o = t * 256
            part[step, h, t] = both[0:T, o : o + 128] + (
                both[0:T, o + 128 : o + 256] + both[T : 2 * T, o : o + 128] + both[T : 2 * T, o + 128 : o + 256]
            )

        def to(t):
            send(
                part.at[step, h, t], part_in.at[step, h, j], pt_s.at[step, h, t], pt_r.at[step, h, j],
                at((z % 2) * 2 + t, y, (z + spread) % 4, x % 2),
            )

        for t in range(2):
            here = self_part & (x == t)

            @pl.when(here)
            def _():
                part_in[step, h, j] = part[step, h, t]

            @pl.when(jnp.logical_not(here))
            def _():
                to(t)

    def drain_part(step, h):
        for t in range(2):

            @pl.when(jnp.logical_not(self_part & (x == t)))
            def _():
                wait_send(part.at[step, h, t], pt_s.at[step, h, t])

    def send_solution(step, h):
        for k in range(2):

            @pl.when(jnp.logical_not(self_part & (j == k)))
            def _():
                wait_recv(part_in.at[step, h, k], pt_r.at[step, h, k])

        sol[step, h, sol_slot] = part_in[step, h, 0] + part_in[step, h, 1]
        mine = sol.at[step, h, sol_slot]
        if step + 1 < STEPS:

            def one(index):
                other = (9 + index) % 15 + 1
                send(
                    mine, mine, g2_s.at[step, h], g2_r.at[step, h],
                    at(x, (y + other // 4) % 4, (z + other % 4) % 4, j),
                )

            loop(0, 15, one)
        rows = pl.ds(pl.multiple_of(q_here * 64 + h * T, T), T)
        for hop in (2, 1, 3):
            send(mine, done.at[step, rows], ot_s.at[step, h], ot_r.at[step], at((x + hop) % 4, y, z_row, x % 2))

        @pl.when(self_out)
        def _():
            done[step, rows] = sol[step, h, sol_slot]

        @pl.when(jnp.logical_not(self_out))
        def _():
            send(mine, done.at[step, rows], ot_s.at[step, h], ot_r.at[step], at(x, y, z_row, x % 2))

    def drain_solution(step, h):
        if step + 1 < STEPS:
            wait_send(sol.at[step, h, pl.ds(0, 15)], g2_s.at[step, h])

        @pl.when(self_out)
        def _():
            wait_send(sol.at[step, h, pl.ds(0, 3)], ot_s.at[step, h])

        @pl.when(jnp.logical_not(self_out))
        def _():
            wait_send(sol.at[step, h, pl.ds(0, 4)], ot_s.at[step, h])

    def gather_solution(step, h):
        wait_recv(sol.at[step, h, pl.ds(0, 15)], g2_r.at[step, h])
        for g in range(2):
            for b in range(GROUPS):
                high, low = halves(sol[step, h, g * 8 + b])
                a_sol[h, g * T : (g + 1) * T, b * 128 : (b + 1) * 128] = high
                a_sol[h, 2 * T + g * T : 2 * T + (g + 1) * T, b * 128 : (b + 1) * 128] = low

    def update(step, later_step, h):
        both = dot(a_sol[h], u_parts[SLOT[later_step, step]])
        for t in range(2):
            o = t * 256
            total = both[0 : 2 * T, o : o + 128] + (
                both[0 : 2 * T, o + 128 : o + 256]
                + both[2 * T : 4 * T, o : o + 128]
                + both[2 * T : 4 * T, o + 128 : o + 256]
            )
            if step > 0:
                total = total + later[later_step - 2, h, t]
            if later_step > step + 1:
                later[later_step - 2, h, t] = total
            else:
                for g in range(2):
                    upd[step, h, t, g] = -total[g * T : (g + 1) * T]
        if later_step > step + 1:
            return
        for t in range(2):
            for g in range(2):
                here = (x == 2 * g + j) & (j == t)

                @pl.when(here)
                def _():
                    upd_in[step, h, x] = upd[step, h, t, g]

                @pl.when(jnp.logical_not(here))
                def _():
                    send(
                        upd.at[step, h, t, g], upd_in.at[step, h, x], up_s.at[step, h], up_r.at[step, h],
                        at(2 * g + j, y, z, t),
                    )

    def drain_update(step, h):
        @pl.when(self_upd)
        def _():
            wait_send(upd_in.at[step, h, pl.ds(0, 3)], up_s.at[step, h])

        @pl.when(jnp.logical_not(self_upd))
        def _():
            wait_send(upd_in.at[step, h], up_s.at[step, h])

    def write(step):
        @pl.when(self_out)
        def _():
            wait_recv(done.at[step, pl.ds(0, 6 * T)], ot_r.at[step])

        @pl.when(jnp.logical_not(self_out))
        def _():
            wait_recv(done.at[step], ot_r.at[step])

        turned[step] = done[step].T
        pltpu.make_async_copy(turned.at[step], out.at[step], wr.at[step]).start()

    barrier = pltpu.get_barrier_semaphore()

    def greet(device):
        pl.semaphore_signal(barrier, inc=1, device_id=device, device_id_type=MESH)

    pltpu.make_async_copy(earlier, y_raw, ld.at[0]).start()
    load_known(0)
    pltpu.make_async_copy(rhs, b_raw, ld.at[1]).start()
    load_inverse(0)

    def greet_plane(other):
        greet(at(x, (y + other // 4) % 4, (z + other % 4) % 4, j))

    loop(1, 16, greet_plane)
    for hop in range(4):
        for core in range(2):
            if (hop, core) != (0, 0):
                greet(at((x + hop) % 4, y, z, (j + core) % 2))
            greet(at((x + hop) % 4, y, (z + 1) % 4, (j + core) % 2))
            greet(at((x + hop) % 4, y, (z + 3) % 4, (j + core) % 2))
    a_res[...] = jnp.zeros_like(a_res)
    wait_local(y_raw, ld.at[0])

    def split_earlier(group):
        rows = pl.ds(pl.multiple_of(group * 128, 128), 128)
        high, low = halves(y_raw[group])
        y_parts[rows, 0:256] = high
        y_parts[rows, 256:512] = low

    loop(0, KNOWN, split_earlier)
    wait_local(b_raw, ld.at[1])
    known_terms(0)
    pl.semaphore_wait(barrier, 15 + 7 + 16)
    send_known(0)
    share_inverse(0)
    load_update(PAIRS[0])
    load_known(1)
    share_update(PAIRS[0])
    load_known(2)
    load_known(3)
    collect_known(0)
    for h in range(CHAINS):
        send_residual(0, h)
    prepare_inverse(0)
    for step in range(1, STEPS):
        load_inverse(step)
    for pair in PAIRS[1:]:
        load_update(pair)

    for step in range(STEPS):
        for h in range(CHAINS):
            solve(step, h)
        if step == 0:
            prepare_update(PAIRS[0])
            known_terms(1)
            send_known(1)
        elif step + 1 < STEPS:
            for h in range(CHAINS):
                drain_residual(step - 1, h)
                drain_solution(step - 1, h)
                drain_part(step - 1, h)
        for h in range(CHAINS):
            send_solution(step, h)
        if step + 1 == STEPS:
            break
        if step == 0:
            share_inverse(1)
            for pair in PAIRS[1:]:
                share_update(pair)
            known_terms(2)
            send_known(2)
            known_terms(3)
            send_known(3)
            collect_known(1)
            prepare_update((2, 0))
            prepare_update((3, 0))
        elif step == 1:
            share_inverse(3)
            prepare_inverse(2)
        for h in range(CHAINS):
            gather_solution(step, h)
            update(step, step + 1, h)
        for later_step in range(step + 2, STEPS):
            for h in range(CHAINS):
                update(step, later_step, h)
        if step == 0:
            share_inverse(2)
            collect_known(2)
            collect_known(3)
        for h in range(CHAINS):
            send_residual(step + 1, h)
        if step == 0:
            prepare_inverse(1)
            prepare_update((2, 1))
            prepare_update((3, 1))
        elif step == 1:
            prepare_inverse(3)
            prepare_update((3, 2))
        write(step)
        for h in range(CHAINS):
            drain_update(step, h)

    for step in range(STEPS):
        wait_send(known.at[step, pl.ds(0, 192)], kn_s.at[step])
        wait_send(i_raw.at[step, j], sib_s.at[step])
    for slot in range(len(PAIRS)):
        wait_send(u_raw.at[slot, j], sib_s.at[4 + slot])
    for step in range(STEPS - 2, STEPS):
        for h in range(CHAINS):
            drain_residual(step, h)
            drain_part(step, h)
            drain_solution(step, h)
    write(STEPS - 1)
    for step in range(STEPS):
        wait_local(turned.at[step], wr.at[step])


def per_device(factor, earlier, rhs, inverse):
    dma = pltpu.SemaphoreType.DMA
    vmem = pltpu.VMEM
    updates = len(PAIRS)
    return pl.pallas_call(
        kernel,
        out_shape=jax.ShapeDtypeStruct(rhs.shape, F32),
        in_specs=[pl.BlockSpec(memory_space=pl.ANY)] * 4,
        out_specs=pl.BlockSpec(memory_space=pl.ANY),
        scratch_shapes=[
            vmem((KNOWN, 128, 256), F32),
            vmem((KNOWN * 128, 512), BF16),
            vmem((STEPS, KNOWN, 128, 128), F32),
            vmem((256, KNOWN * 128), BF16),
            vmem((updates, 2, GROUPS, 128, 128), F32),
            vmem((updates, GROUPS * 128, 512), BF16),
            vmem((STEPS, 2, 16, 128, 128), F32),
            vmem((STEPS, 2048, 512), BF16),
            vmem((STEPS, 128, 256), F32),
            vmem((256, 128), F32),
            vmem((STEPS, 256, 128), F32),
            vmem((STEPS, 4, 64, 128), F32),
            vmem((STEPS, CHAINS, T, 128), F32),
            vmem((STEPS, CHAINS, 16, T, 128), F32),
            vmem((STEPS, CHAINS, 16, T, 128), F32),
            vmem((STEPS - 1, CHAINS, 4, T, 128), F32),
            vmem((STEPS, CHAINS, 2, T, 128), F32),
            vmem((STEPS, CHAINS, 2, T, 128), F32),
            vmem((STEPS - 1, CHAINS, 2, 2, T, 128), F32),
            vmem((2, CHAINS, 2, 2 * T, 128), F32),
            vmem((STEPS, 256, 128), F32),
            vmem((STEPS, 128, 256), F32),
            vmem((CHAINS, 2 * T, 2048), BF16),
            vmem((CHAINS, 4 * T, 1024), BF16),
            dma((16,)),
            dma((10,)),
            dma((10,)),
            dma((STEPS,)),
            dma((STEPS,)),
            dma((STEPS, CHAINS, 16)),
            dma((STEPS, CHAINS, 16)),
            dma((STEPS, CHAINS, 2)),
            dma((STEPS, CHAINS, 2)),
            dma((STEPS, CHAINS)),
            dma((STEPS, CHAINS)),
            dma((STEPS, CHAINS)),
            dma((STEPS,)),
            dma((STEPS, CHAINS)),
            dma((STEPS, CHAINS)),
            dma((STEPS,)),
        ],
        compiler_params=pltpu.CompilerParams(
            collective_id=0, has_side_effects=True, vmem_limit_bytes=60 * 1024 * 1024
        ),
        cost_estimate=pl.CostEstimate(flops=6_000_000_000, bytes_accessed=20_000_000, transcendentals=0),
        name="substitution",
    )(jnp.transpose(factor, (0, 2, 1, 3)), earlier, rhs, inverse)


def solution(mesh):
    return jax.shard_map(
        per_device,
        mesh=mesh,
        in_specs=(
            P(None, "row", None, "col"),
            P(None, "col", None),
            P(None, "row", None),
            P(None, "row", None),
        ),
        out_specs=P(None, "row", None),
        check_vma=False,
    )
```

```python
import functools

import jax
import jax.numpy as jnp
from jax import lax
from jax.experimental import pallas as pl
from jax.experimental.pallas import tpu as pltpu
from jax.sharding import PartitionSpec as P

F32 = jnp.float32
BF16 = jnp.bfloat16
MESH = pl.DeviceIdType.MESH
STEPS = 4
KNOWN = 20
GROUPS = 8
CHAINS = 2
T = 32
PLANE = [(2, 2), (2, 1), (2, 3), (1, 2), (3, 2), (2, 0), (0, 2), (1, 1), (1, 3), (3, 1), (3, 3), (1, 0), (3, 0), (0, 1), (0, 3)]
PAIRS = [(1, 0), (2, 0), (2, 1), (3, 0), (3, 1), (3, 2)]
SLOT = {pair: index for index, pair in enumerate(PAIRS)}


def halves(value):
    high = value.astype(BF16)
    return high, (value - high.astype(F32)).astype(BF16)


def dot(left, right):
    return lax.dot_general(left, right, (((1,), (0,)), ((), ())), preferred_element_type=F32)


def kernel(
    factor, earlier, rhs, inverse, out,
    y_raw, y_parts, f_raw, f_parts, u_raw, u_parts, i_raw, i_parts, b_raw, b_turn,
    known, known_in, start, res, sol, upd_in, part_in, part, upd, later, done, turned, last_in, a_res, a_sol,
    ld, sib_s, sib_r, kn_s, kn_r, g1_s, g1_r, pt_s, pt_r, g2_s, g2_r, ot_s, ot_r, up_s, up_r, ls_s, ls_r, wr,
):
    row = lax.axis_index("row")
    x = lax.axis_index("col")
    y, z, j = row // 8, (row // 2) % 4, row % 2
    m = row // 2

    def at(x_, y_, z_, j_):
        return ((y_ * 4 + z_) * 2 + j_, x_)

    sibling = at(x, y, z, 1 - j)
    own_zone = (z % 2) == (x // 2)
    g_here = jnp.where(own_zone, 0, 1)
    z_row = jnp.where(own_zone, z, (z + 3) % 4)
    q_here = (x + 2 * j + g_here) % 4
    sol_slot = g_here * 8 + y * 2 + z_row // 2
    self_part = own_zone & (j == 0)
    self_out = own_zone & (x % 2 == j)
    self_upd = j == 0

    def send(src, dst, ss, rs, device):
        pltpu.make_async_remote_copy(
            src_ref=src, dst_ref=dst, send_sem=ss, recv_sem=rs, device_id=device, device_id_type=MESH
        ).start()

    def wait_recv(ref, sem):
        pltpu.make_async_remote_copy(
            src_ref=ref, dst_ref=ref, send_sem=sem, recv_sem=sem, device_id=sibling, device_id_type=MESH
        ).wait_recv()

    def wait_send(ref, sem):
        pltpu.make_async_remote_copy(
            src_ref=ref, dst_ref=ref, send_sem=sem, recv_sem=sem, device_id=sibling, device_id_type=MESH
        ).wait_send()

    def wait_local(ref, sem):
        pltpu.make_async_copy(ref, ref, sem).wait()

    def loop(lo, hi, body):
        lax.fori_loop(lo, hi, lambda index, carry: (body(index), carry)[1], 0)

    def load_known(step):
        pltpu.make_async_copy(factor.at[step, pl.ds(0, KNOWN)], f_raw.at[step], ld.at[16 + step]).start()

    def load_inverse(step):
        def one(tile):
            lanes = pl.ds(pl.multiple_of((2 * tile + j) * 128, 128), 128)
            pltpu.make_async_copy(inverse.at[step, :, lanes], i_raw.at[step, j, tile], ld.at[6 + step]).start()

        loop(0, 16, one)

    def share_inverse(step):
        def one(tile):
            lanes = pl.ds(pl.multiple_of((2 * tile + 1 - j) * 128, 128), 128)
            send(inverse.at[step, :, lanes], i_raw.at[step, j, tile], sib_s.at[step], sib_r.at[step], sibling)

        loop(0, 16, one)

    def load_update(pair):
        later_step, step = pair
        slot = SLOT[pair]
        groups = pl.ds(KNOWN + step * GROUPS, GROUPS)
        pltpu.make_async_copy(factor.at[later_step, groups], u_raw.at[slot, j], ld.at[10 + slot]).start()

    def share_update(pair):
        slot = SLOT[pair]
        wait_local(u_raw.at[slot, j], ld.at[10 + slot])
        send(u_raw.at[slot, j], u_raw.at[slot, j], sib_s.at[4 + slot], sib_r.at[4 + slot], sibling)

    def prepare_inverse(step):
        wait_local(i_raw.at[step, j], ld.at[6 + step])
        wait_recv(i_raw.at[step, 1 - j], sib_r.at[step])

        def one(tile):
            rows = pl.ds(pl.multiple_of(tile * 128, 128), 128)
            for t in range(2):
                high, low = halves(i_raw[step, t, tile])
                i_parts[step, rows, t * 256 : t * 256 + 128] = high.T
                i_parts[step, rows, t * 256 + 128 : t * 256 + 256] = low.T

        loop(0, 16, one)

    def prepare_update(pair):
        slot = SLOT[pair]
        wait_recv(u_raw.at[slot, 1 - j], sib_r.at[4 + slot])

        def one(group):
            rows = pl.ds(pl.multiple_of(group * 128, 128), 128)
            for t in range(2):
                high, low = halves(u_raw[slot, t, group])
                u_parts[slot, rows, t * 256 : t * 256 + 128] = high.T
                u_parts[slot, rows, t * 256 + 128 : t * 256 + 256] = low.T

        loop(0, GROUPS, one)

    def split_known(step, first, end):
        def one(group):
            lanes = pl.ds(pl.multiple_of(group * 128, 128), 128)
            high, low = halves(f_raw[step, group])
            f_parts[0:128, lanes] = high
            f_parts[128:256, lanes] = low

        loop(first, end, one)

    def known_terms(step):
        if step > 0:
            wait_local(f_raw.at[step], ld.at[16 + step])
            split_known(step, 0, KNOWN)
        both = dot(f_parts[...], y_parts[...])
        total = both[0:128, 0:256] + (both[0:128, 256:512] + both[128:256, 0:256] + both[128:256, 256:512])
        known[step] = -(total.T)
        b_turn[...] = b_raw[step].T
        mine = pl.ds(pl.multiple_of(x * 64, 64), 64)
        known_in[step, x] = b_turn[mine] + known[step, mine]

    def send_known(step):
        for hop in (2, 1, 3):
            q = (x + hop) % 4
            rows = pl.ds(pl.multiple_of(q * 64, 64), 64)
            send(known.at[step, rows], known_in.at[step, x], kn_s.at[step], kn_r.at[step], at(q, y, z, j))

    def collect_known(step):
        wait_recv(known_in.at[step, pl.ds(0, 3)], kn_r.at[step])
        total = known_in[step, 0] + known_in[step, 1] + known_in[step, 2] + known_in[step, 3]
        for h in range(CHAINS):
            start[step, h] = total[h * T : (h + 1) * T]

    def send_residual(step, h):
        if step == 0:
            res[step, h, m] = start[step, h]
        else:

            @pl.when(self_upd)
            def _():
                wait_recv(upd_in.at[step - 1, h, pl.ds(0, 3)], up_r.at[step - 1, h])

            @pl.when(jnp.logical_not(self_upd))
            def _():
                wait_recv(upd_in.at[step - 1, h], up_r.at[step - 1, h])

            res[step, h, m] = start[step, h] + (
                upd_in[step - 1, h, 0] + upd_in[step - 1, h, 1] + upd_in[step - 1, h, 2] + upd_in[step - 1, h, 3]
            )

        def one(other):
            send(
                res.at[step, h, m], res.at[step, h, m], g1_s.at[step, h, other], g1_r.at[step, h, m],
                at(x, other // 4, other % 4, j),
            )

        loop(m + 1, 16, one)

    def drain_residual(step, h):
        def one(other):
            wait_send(res.at[step, h, m], g1_s.at[step, h, other])

        loop(m + 1, 16, one)

    def solve(step, h):
        def arrived(tile):
            wait_recv(res.at[step, h, tile], g1_r.at[step, h, tile])

        loop(0, m, arrived)
        for tile in range(16):
            high, low = halves(res[step, h, tile])
            a_res[h, 0:T, tile * 128 : (tile + 1) * 128] = high
            a_res[h, T : 2 * T, tile * 128 : (tile + 1) * 128] = low
        both = dot(a_res[h], i_parts[step])
        for t in range(2):
            o = t * 256
            part[step, h, t] = both[0:T, o : o + 128] + (
                both[0:T, o + 128 : o + 256] + both[T : 2 * T, o : o + 128] + both[T : 2 * T, o + 128 : o + 256]
            )

        if step + 1 == STEPS:
            send_last(h)
            return

        def to(t):
            column = (z % 2) * 2 + t
            distance = (x + 4 - column) % 4
            send(
                part.at[step, h, t], part_in.at[step, h, j], pt_s.at[step, h, t], pt_r.at[step, h, j],
                at(column, y, (z + distance % 2) % 4, distance // 2),
            )

        for t in range(2):
            here = self_part & (x % 2 == t)

            @pl.when(here)
            def _():
                part_in[step, h, j] = part[step, h, t]

            @pl.when(jnp.logical_not(here))
            def _():
                to(t)

    def send_last(h):
        for t in range(2):
            for hop in (2, 1, 3):
                send(
                    part.at[STEPS - 1, h, t], last_in.at[h, x, j], ls_s.at[h], ls_r.at[h], at((x + hop) % 4, y, z, t)
                )
        last_in[h, x, j] = part[STEPS - 1, h, j]
        send(part.at[STEPS - 1, h, 1 - j], last_in.at[h, x, j], ls_s.at[h], ls_r.at[h], sibling)

    def collect_last(h):
        wait_recv(res.at[0, h, pl.ds(0, 7)], ls_r.at[h])
        for q in range(4):
            done[STEPS - 1, q * 64 + h * T : q * 64 + (h + 1) * T] = last_in[h, q, 0] + last_in[h, q, 1]

    def drain_last(h):
        wait_send(res.at[0, h, pl.ds(0, 7)], ls_s.at[h])

    def drain_part(step, h):
        for t in range(2):

            @pl.when(jnp.logical_not(self_part & (x % 2 == t)))
            def _():
                wait_send(part.at[step, h, t], pt_s.at[step, h, t])

    def send_solution(step, h):
        for k in range(2):

            @pl.when(jnp.logical_not(self_part & (j == k)))
            def _():
                wait_recv(part_in.at[step, h, k], pt_r.at[step, h, k])

        sol[step, h, sol_slot] = part_in[step, h, 0] + part_in[step, h, 1]
        mine = sol.at[step, h, sol_slot]
        for dy, dz in PLANE:
            send(mine, mine, g2_s.at[step, h], g2_r.at[step, h], at(x, (y + dy) % 4, (z + dz) % 4, j))
        rows = pl.ds(pl.multiple_of(q_here * 64 + h * T, T), T)
        for hop in (2, 1, 3):
            send(mine, done.at[step, rows], ot_s.at[step, h], ot_r.at[step], at((x + hop) % 4, y, z_row, x % 2))

        @pl.when(self_out)
        def _():
            done[step, rows] = sol[step, h, sol_slot]

        @pl.when(jnp.logical_not(self_out))
        def _():
            send(mine, done.at[step, rows], ot_s.at[step, h], ot_r.at[step], at(x, y, z_row, x % 2))

    def drain_solution(step, h):
        wait_send(sol.at[step, h, pl.ds(0, 15)], g2_s.at[step, h])

        @pl.when(self_out)
        def _():
            wait_send(sol.at[step, h, pl.ds(0, 3)], ot_s.at[step, h])

        @pl.when(jnp.logical_not(self_out))
        def _():
            wait_send(sol.at[step, h, pl.ds(0, 4)], ot_s.at[step, h])

    def gather_solution(step, h):
        wait_recv(sol.at[step, h, pl.ds(0, 15)], g2_r.at[step, h])
        for g in range(2):
            for b in range(GROUPS):
                high, low = halves(sol[step, h, g * 8 + b])
                a_sol[h, g * T : (g + 1) * T, b * 128 : (b + 1) * 128] = high
                a_sol[h, 2 * T + g * T : 2 * T + (g + 1) * T, b * 128 : (b + 1) * 128] = low

    def update(step, later_step, h):
        both = dot(a_sol[h], u_parts[SLOT[later_step, step]])
        for t in range(2):
            o = t * 256
            total = both[0 : 2 * T, o : o + 128] + (
                both[0 : 2 * T, o + 128 : o + 256]
                + both[2 * T : 4 * T, o : o + 128]
                + both[2 * T : 4 * T, o + 128 : o + 256]
            )
            if step > 0:
                total = total + later[later_step - 2, h, t]
            if later_step > step + 1:
                later[later_step - 2, h, t] = total
            else:
                for g in range(2):
                    upd[step, h, t, g] = -total[g * T : (g + 1) * T]
        if later_step > step + 1:
            return
        for t in range(2):
            for g in range(2):
                here = (j == 0) & (g == 0) & (t == 0)

                @pl.when(here)
                def _():
                    upd_in[step, h, x] = upd[step, h, t, g]

                @pl.when(jnp.logical_not(here))
                def _():
                    send(
                        upd.at[step, h, t, g], upd_in.at[step, h, x], up_s.at[step, h], up_r.at[step, h],
                        at((x + 2 * j + g) % 4, y, z, t),
                    )

    def drain_update(step, h):
        @pl.when(self_upd)
        def _():
            wait_send(upd_in.at[step, h, pl.ds(0, 3)], up_s.at[step, h])

        @pl.when(jnp.logical_not(self_upd))
        def _():
            wait_send(upd_in.at[step, h], up_s.at[step, h])

    def collect_done(step):
        @pl.when(self_out)
        def _():
            wait_recv(done.at[step, pl.ds(0, 6 * T)], ot_r.at[step])

        @pl.when(jnp.logical_not(self_out))
        def _():
            wait_recv(done.at[step], ot_r.at[step])

    def write(step):
        turned[step] = done[step].T
        pltpu.make_async_copy(turned.at[step], out.at[step], wr.at[step]).start()

    barrier = pltpu.get_barrier_semaphore()

    def greet(device):
        pl.semaphore_signal(barrier, inc=1, device_id=device, device_id_type=MESH)

    half = KNOWN // 2
    for part_of in range(2):
        groups = pl.ds(part_of * half, half)
        pltpu.make_async_copy(earlier.at[groups], y_raw.at[groups], ld.at[part_of]).start()
        pltpu.make_async_copy(factor.at[0, groups], f_raw.at[0, groups], ld.at[2 + part_of]).start()
    pltpu.make_async_copy(rhs, b_raw, ld.at[16]).start()

    def greet_plane(other):
        greet(at(x, (y + other // 4) % 4, (z + other % 4) % 4, j))

    for hop in range(4):
        for core in range(2):
            if (hop, core) != (0, 0):
                greet(at((x + hop) % 4, y, z, (j + core) % 2))
            greet(at((x + hop) % 4, y, (z + 1) % 4, (j + core) % 2))
            greet(at((x + hop) % 4, y, (z + 3) % 4, (j + core) % 2))
    loop(1, 16, greet_plane)
    load_inverse(0)
    load_update(PAIRS[0])
    load_known(1)

    def clear(tile):
        for step in range(STEPS):
            for h in range(CHAINS):
                res[step, h, tile] = jnp.zeros((T, 128), F32)

    loop(m + 1, 16, clear)

    def split_earlier(group):
        rows = pl.ds(pl.multiple_of(group * 128, 128), 128)
        high, low = halves(y_raw[group])
        y_parts[rows, 0:256] = high
        y_parts[rows, 256:512] = low

    for part_of in range(2):
        groups = pl.ds(part_of * half, half)
        wait_local(y_raw.at[groups], ld.at[part_of])
        loop(part_of * half, (part_of + 1) * half, split_earlier)
        wait_local(f_raw.at[0, groups], ld.at[2 + part_of])
        split_known(0, part_of * half, (part_of + 1) * half)
    wait_local(b_raw, ld.at[16])
    known_terms(0)
    pl.semaphore_wait(barrier, 15 + 7 + 16)
    send_known(0)
    share_inverse(0)
    share_update(PAIRS[0])
    for step in range(2, STEPS):
        load_known(step)
    collect_known(0)
    for h in range(CHAINS):
        send_residual(0, h)
    prepare_inverse(0)
    for step in range(1, STEPS):
        load_inverse(step)
    for pair in PAIRS[1:]:
        load_update(pair)

    for step in range(STEPS):
        for h in range(CHAINS):
            solve(step, h)
        if step + 1 == STEPS:
            break
        if step == 0:
            prepare_update(PAIRS[0])
            known_terms(1)
            send_known(1)
        for h in range(CHAINS):
            send_solution(step, h)
        if step == 0:
            share_inverse(1)
            for pair in PAIRS[1:]:
                share_update(pair)
            known_terms(2)
            send_known(2)
            collect_known(1)
        elif step == 1:
            share_inverse(3)
            prepare_inverse(2)
        for h in range(CHAINS):
            drain_part(step, h)
        for h in range(CHAINS):
            gather_solution(step, h)
            update(step, step + 1, h)
        if step == 0:
            prepare_update((2, 0))
            prepare_update((3, 0))
        for later_step in range(step + 2, STEPS):
            for h in range(CHAINS):
                update(step, later_step, h)
        if step == 0:
            share_inverse(2)
        for h in range(CHAINS):
            send_residual(step + 1, h)
        if step == 0:
            prepare_inverse(1)
            known_terms(3)
            send_known(3)
            collect_known(2)
            prepare_update((2, 1))
            prepare_update((3, 1))
        elif step == 1:
            prepare_inverse(3)
            prepare_update((3, 2))
            collect_known(3)
        collect_done(step)
        write(step)
        for h in range(CHAINS):
            drain_update(step, h)
            drain_residual(step, h)
            drain_solution(step, h)

    for step in range(STEPS):
        wait_send(known.at[step, pl.ds(0, 192)], kn_s.at[step])
        wait_send(i_raw.at[step, j], sib_s.at[step])
    for slot in range(len(PAIRS)):
        wait_send(u_raw.at[slot, j], sib_s.at[4 + slot])
    for h in range(CHAINS):
        drain_residual(STEPS - 1, h)
    for h in range(CHAINS):
        collect_last(h)
    write(STEPS - 1)
    for h in range(CHAINS):
        drain_last(h)
    for step in range(STEPS):
        wait_local(turned.at[step], wr.at[step])


def per_device(factor, earlier, rhs, inverse):
    dma = pltpu.SemaphoreType.DMA
    vmem = pltpu.VMEM
    updates = len(PAIRS)
    return pl.pallas_call(
        kernel,
        out_shape=jax.ShapeDtypeStruct(rhs.shape, F32),
        in_specs=[pl.BlockSpec(memory_space=pl.ANY)] * 4,
        out_specs=pl.BlockSpec(memory_space=pl.ANY),
        scratch_shapes=[
            vmem((KNOWN, 128, 256), F32),
            vmem((KNOWN * 128, 512), BF16),
            vmem((STEPS, KNOWN, 128, 128), F32),
            vmem((256, KNOWN * 128), BF16),
            vmem((updates, 2, GROUPS, 128, 128), F32),
            vmem((updates, GROUPS * 128, 512), BF16),
            vmem((STEPS, 2, 16, 128, 128), F32),
            vmem((STEPS, 2048, 512), BF16),
            vmem((STEPS, 128, 256), F32),
            vmem((256, 128), F32),
            vmem((STEPS, 256, 128), F32),
            vmem((STEPS, 4, 64, 128), F32),
            vmem((STEPS, CHAINS, T, 128), F32),
            vmem((STEPS, CHAINS, 16, T, 128), F32),
            vmem((STEPS, CHAINS, 16, T, 128), F32),
            vmem((STEPS - 1, CHAINS, 4, T, 128), F32),
            vmem((STEPS, CHAINS, 2, T, 128), F32),
            vmem((STEPS, CHAINS, 2, T, 128), F32),
            vmem((STEPS - 1, CHAINS, 2, 2, T, 128), F32),
            vmem((2, CHAINS, 2, 2 * T, 128), F32),
            vmem((STEPS, 256, 128), F32),
            vmem((STEPS, 128, 256), F32),
            vmem((CHAINS, 4, 2, T, 128), F32),
            vmem((CHAINS, 2 * T, 2048), BF16),
            vmem((CHAINS, 4 * T, 1024), BF16),
            dma((20,)),
            dma((10,)),
            dma((10,)),
            dma((STEPS,)),
            dma((STEPS,)),
            dma((STEPS, CHAINS, 16)),
            dma((STEPS, CHAINS, 16)),
            dma((STEPS, CHAINS, 2)),
            dma((STEPS, CHAINS, 2)),
            dma((STEPS, CHAINS)),
            dma((STEPS, CHAINS)),
            dma((STEPS, CHAINS)),
            dma((STEPS,)),
            dma((STEPS, CHAINS)),
            dma((STEPS, CHAINS)),
            dma((CHAINS,)),
            dma((CHAINS,)),
            dma((STEPS,)),
        ],
        compiler_params=pltpu.CompilerParams(
            collective_id=0, has_side_effects=True, vmem_limit_bytes=60 * 1024 * 1024
        ),
        cost_estimate=pl.CostEstimate(flops=6_000_000_000, bytes_accessed=20_000_000, transcendentals=0),
        name="substitution",
    )(jnp.transpose(factor, (0, 2, 1, 3)), earlier, rhs, inverse)


def solution(mesh):
    return jax.shard_map(
        per_device,
        mesh=mesh,
        in_specs=(
            P(None, "row", None, "col"),
            P(None, "col", None),
            P(None, "row", None),
            P(None, "row", None),
        ),
        out_specs=P(None, "row", None),
        check_vma=False,
    )
```

```python
import functools

import jax
import jax.numpy as jnp
from jax import lax
from jax.experimental import pallas as pl
from jax.experimental.pallas import tpu as pltpu
from jax.sharding import PartitionSpec as P

F32 = jnp.float32
BF16 = jnp.bfloat16
MESH = pl.DeviceIdType.MESH
STEPS = 4
KNOWN = 20
GROUPS = 8
CHAINS = 2
T = 32
PLANE = [(2, 2), (2, 1), (2, 3), (1, 2), (3, 2), (2, 0), (0, 2), (1, 1), (1, 3), (3, 1), (3, 3), (1, 0), (3, 0), (0, 1), (0, 3)]
PAIRS = [(1, 0), (2, 0), (2, 1), (3, 0), (3, 1), (3, 2)]
SLOT = {pair: index for index, pair in enumerate(PAIRS)}


def halves(value):
    high = value.astype(BF16)
    return high, (value - high.astype(F32)).astype(BF16)


def dot(left, right):
    return lax.dot_general(left, right, (((1,), (0,)), ((), ())), preferred_element_type=F32)


def kernel(
    factor, earlier, rhs, inverse, out,
    y_raw, y_parts, f_raw, f_parts, u_raw, u_parts, i_raw, i_parts, b_raw, b_turn,
    known, known_in, start, res, sol, upd_in, part_in, part, upd, later, done, turned, last_in, a_res, a_sol,
    ld, sib_s, sib_r, kn_s, kn_r, g1_s, g1_r, pt_s, pt_r, g2_s, g2_r, ot_s, ot_r, up_s, up_r, ls_s, ls_r, wr,
):
    row = lax.axis_index("row")
    x = lax.axis_index("col")
    y, z, j = row // 8, (row // 2) % 4, row % 2
    m = row // 2

    def at(x_, y_, z_, j_):
        return ((y_ * 4 + z_) * 2 + j_, x_)

    sibling = at(x, y, z, 1 - j)
    own_zone = (z % 2) == (x // 2)
    g_here = jnp.where(own_zone, 0, 1)
    z_row = jnp.where(own_zone, z, (z + 3) % 4)
    q_here = (x + 2 * j + g_here) % 4
    sol_slot = g_here * 8 + y * 2 + z_row // 2
    self_part = own_zone & (j == 0)
    self_out = own_zone & (x % 2 == j)
    self_upd = j == 0

    def send(src, dst, ss, rs, device):
        pltpu.make_async_remote_copy(
            src_ref=src, dst_ref=dst, send_sem=ss, recv_sem=rs, device_id=device, device_id_type=MESH
        ).start()

    def wait_recv(ref, sem):
        pltpu.make_async_remote_copy(
            src_ref=ref, dst_ref=ref, send_sem=sem, recv_sem=sem, device_id=sibling, device_id_type=MESH
        ).wait_recv()

    def wait_send(ref, sem):
        pltpu.make_async_remote_copy(
            src_ref=ref, dst_ref=ref, send_sem=sem, recv_sem=sem, device_id=sibling, device_id_type=MESH
        ).wait_send()

    def wait_local(ref, sem):
        pltpu.make_async_copy(ref, ref, sem).wait()

    def loop(lo, hi, body):
        lax.fori_loop(lo, hi, lambda index, carry: (body(index), carry)[1], 0)

    def load_known(step):
        pltpu.make_async_copy(factor.at[step, pl.ds(0, KNOWN)], f_raw.at[step], ld.at[16 + step]).start()

    def load_inverse(step):
        def one(tile):
            lanes = pl.ds(pl.multiple_of((2 * tile + j) * 128, 128), 128)
            pltpu.make_async_copy(inverse.at[step, :, lanes], i_raw.at[step, j, tile], ld.at[6 + step]).start()

        loop(0, 16, one)

    def share_inverse(step):
        def one(tile):
            lanes = pl.ds(pl.multiple_of((2 * tile + 1 - j) * 128, 128), 128)
            send(inverse.at[step, :, lanes], i_raw.at[step, j, tile], sib_s.at[step], sib_r.at[step], sibling)

        loop(0, 16, one)

    def load_update(pair):
        later_step, step = pair
        slot = SLOT[pair]
        groups = pl.ds(KNOWN + step * GROUPS, GROUPS)
        pltpu.make_async_copy(factor.at[later_step, groups], u_raw.at[slot, j], ld.at[10 + slot]).start()

    def share_update(pair):
        slot = SLOT[pair]
        wait_local(u_raw.at[slot, j], ld.at[10 + slot])
        send(u_raw.at[slot, j], u_raw.at[slot, j], sib_s.at[4 + slot], sib_r.at[4 + slot], sibling)

    def prepare_inverse(step):
        wait_local(i_raw.at[step, j], ld.at[6 + step])
        wait_recv(i_raw.at[step, 1 - j], sib_r.at[step])

        def one(tile):
            rows = pl.ds(pl.multiple_of(tile * 128, 128), 128)
            for t in range(2):
                high, low = halves(i_raw[step, t, tile])
                i_parts[step, rows, t * 256 : t * 256 + 128] = high.T
                i_parts[step, rows, t * 256 + 128 : t * 256 + 256] = low.T

        loop(0, 16, one)

    def prepare_update(pair):
        slot = SLOT[pair]
        wait_recv(u_raw.at[slot, 1 - j], sib_r.at[4 + slot])

        def one(group):
            rows = pl.ds(pl.multiple_of(group * 128, 128), 128)
            for t in range(2):
                high, low = halves(u_raw[slot, t, group])
                u_parts[slot, rows, t * 256 : t * 256 + 128] = high.T
                u_parts[slot, rows, t * 256 + 128 : t * 256 + 256] = low.T

        loop(0, GROUPS, one)

    def split_known(step, first, end):
        def one(group):
            lanes = pl.ds(pl.multiple_of(group * 128, 128), 128)
            high, low = halves(f_raw[step, group])
            f_parts[0:128, lanes] = high
            f_parts[128:256, lanes] = low

        loop(first, end, one)

    def known_terms(step):
        wait_local(f_raw.at[step], ld.at[16 + step])
        split_known(step, 0, KNOWN)
        finish_known(step, dot(f_parts[...], y_parts[...]))

    def finish_known(step, both):
        total = both[0:128, 0:256] + (both[0:128, 256:512] + both[128:256, 0:256] + both[128:256, 256:512])
        known[step] = -(total.T)
        b_turn[...] = b_raw[step].T
        mine = pl.ds(pl.multiple_of(x * 64, 64), 64)
        known_in[step, x] = b_turn[mine] + known[step, mine]

    def send_known(step):
        for hop in (2, 1, 3):
            q = (x + hop) % 4
            rows = pl.ds(pl.multiple_of(q * 64, 64), 64)
            send(known.at[step, rows], known_in.at[step, x], kn_s.at[step], kn_r.at[step], at(q, y, z, j))

    def collect_known(step):
        wait_recv(known_in.at[step, pl.ds(0, 3)], kn_r.at[step])
        total = known_in[step, 0] + known_in[step, 1] + known_in[step, 2] + known_in[step, 3]
        for h in range(CHAINS):
            start[step, h] = total[h * T : (h + 1) * T]

    def send_residual(step, h):
        if step == 0:
            res[step, h, m] = start[step, h]
        else:

            @pl.when(self_upd)
            def _():
                wait_recv(upd_in.at[step - 1, h, pl.ds(0, 3)], up_r.at[step - 1, h])

            @pl.when(jnp.logical_not(self_upd))
            def _():
                wait_recv(upd_in.at[step - 1, h], up_r.at[step - 1, h])

            res[step, h, m] = start[step, h] + (
                upd_in[step - 1, h, 0] + upd_in[step - 1, h, 1] + upd_in[step - 1, h, 2] + upd_in[step - 1, h, 3]
            )

        def one(other):
            send(
                res.at[step, h, m], res.at[step, h, m], g1_s.at[step, h, other], g1_r.at[step, h, m],
                at(x, other // 4, other % 4, j),
            )

        loop(m + 1, 16, one)

    def drain_residual(step, h):
        def one(other):
            wait_send(res.at[step, h, m], g1_s.at[step, h, other])

        loop(m + 1, 16, one)

    def solve(step, h):
        def arrived(tile):
            wait_recv(res.at[step, h, tile], g1_r.at[step, h, tile])

        loop(0, m, arrived)
        for tile in range(16):
            high, low = halves(res[step, h, tile])
            a_res[h, 0:T, tile * 128 : (tile + 1) * 128] = high
            a_res[h, T : 2 * T, tile * 128 : (tile + 1) * 128] = low
        both = dot(a_res[h], i_parts[step])
        for t in range(2):
            o = t * 256
            part[step, h, t] = both[0:T, o : o + 128] + (
                both[0:T, o + 128 : o + 256] + both[T : 2 * T, o : o + 128] + both[T : 2 * T, o + 128 : o + 256]
            )

        if step + 1 == STEPS:
            send_last(h)
            return

        def to(t):
            column = (z % 2) * 2 + t
            distance = (x + 4 - column) % 4
            send(
                part.at[step, h, t], part_in.at[step, h, j], pt_s.at[step, h, t], pt_r.at[step, h, j],
                at(column, y, (z + distance % 2) % 4, distance // 2),
            )

        for t in range(2):
            here = self_part & (x % 2 == t)

            @pl.when(here)
            def _():
                part_in[step, h, j] = part[step, h, t]

            @pl.when(jnp.logical_not(here))
            def _():
                to(t)

    def send_last(h):
        for t in range(2):
            for hop in (2, 1, 3):
                send(
                    part.at[STEPS - 1, h, t], last_in.at[h, x, j], ls_s.at[h], ls_r.at[h], at((x + hop) % 4, y, z, t)
                )
        last_in[h, x, j] = part[STEPS - 1, h, j]
        send(part.at[STEPS - 1, h, 1 - j], last_in.at[h, x, j], ls_s.at[h], ls_r.at[h], sibling)

    def collect_last(h):
        wait_recv(res.at[0, h, pl.ds(0, 7)], ls_r.at[h])
        for q in range(4):
            done[STEPS - 1, q * 64 + h * T : q * 64 + (h + 1) * T] = last_in[h, q, 0] + last_in[h, q, 1]

    def drain_last(h):
        wait_send(res.at[0, h, pl.ds(0, 7)], ls_s.at[h])

    def drain_part(step, h):
        for t in range(2):

            @pl.when(jnp.logical_not(self_part & (x % 2 == t)))
            def _():
                wait_send(part.at[step, h, t], pt_s.at[step, h, t])

    def send_solution(step, h):
        for k in range(2):

            @pl.when(jnp.logical_not(self_part & (j == k)))
            def _():
                wait_recv(part_in.at[step, h, k], pt_r.at[step, h, k])

        sol[step, h, sol_slot] = part_in[step, h, 0] + part_in[step, h, 1]
        mine = sol.at[step, h, sol_slot]
        for dy, dz in PLANE:
            send(mine, mine, g2_s.at[step, h], g2_r.at[step, h], at(x, (y + dy) % 4, (z + dz) % 4, j))

    def send_done(step, h):
        mine = sol.at[step, h, sol_slot]
        rows = pl.ds(pl.multiple_of(q_here * 64 + h * T, T), T)
        for hop in (2, 1, 3):
            send(mine, done.at[step, rows], ot_s.at[step, h], ot_r.at[step], at((x + hop) % 4, y, z_row, x % 2))

        @pl.when(self_out)
        def _():
            done[step, rows] = sol[step, h, sol_slot]

        @pl.when(jnp.logical_not(self_out))
        def _():
            send(mine, done.at[step, rows], ot_s.at[step, h], ot_r.at[step], at(x, y, z_row, x % 2))

    def drain_solution(step, h):
        wait_send(sol.at[step, h, pl.ds(0, 15)], g2_s.at[step, h])

        @pl.when(self_out)
        def _():
            wait_send(sol.at[step, h, pl.ds(0, 3)], ot_s.at[step, h])

        @pl.when(jnp.logical_not(self_out))
        def _():
            wait_send(sol.at[step, h, pl.ds(0, 4)], ot_s.at[step, h])

    def gather_solution(step, h):
        wait_recv(sol.at[step, h, pl.ds(0, 15)], g2_r.at[step, h])
        for g in range(2):
            for b in range(GROUPS):
                high, low = halves(sol[step, h, g * 8 + b])
                a_sol[h, g * T : (g + 1) * T, b * 128 : (b + 1) * 128] = high
                a_sol[h, 2 * T + g * T : 2 * T + (g + 1) * T, b * 128 : (b + 1) * 128] = low

    def update(step, later_step, h):
        both = dot(a_sol[h], u_parts[SLOT[later_step, step]])
        for t in range(2):
            o = t * 256
            total = both[0 : 2 * T, o : o + 128] + (
                both[0 : 2 * T, o + 128 : o + 256]
                + both[2 * T : 4 * T, o : o + 128]
                + both[2 * T : 4 * T, o + 128 : o + 256]
            )
            if step > 0:
                total = total + later[later_step - 2, h, t]
            if later_step > step + 1:
                later[later_step - 2, h, t] = total
            else:
                for g in range(2):
                    upd[step, h, t, g] = -total[g * T : (g + 1) * T]
        if later_step > step + 1:
            return
        for t in range(2):
            for g in range(2):
                here = (j == 0) & (g == 0) & (t == 0)

                @pl.when(here)
                def _():
                    upd_in[step, h, x] = upd[step, h, t, g]

                @pl.when(jnp.logical_not(here))
                def _():
                    send(
                        upd.at[step, h, t, g], upd_in.at[step, h, x], up_s.at[step, h], up_r.at[step, h],
                        at((x + 2 * j + g) % 4, y, z, t),
                    )

    def drain_update(step, h):
        @pl.when(self_upd)
        def _():
            wait_send(upd_in.at[step, h, pl.ds(0, 3)], up_s.at[step, h])

        @pl.when(jnp.logical_not(self_upd))
        def _():
            wait_send(upd_in.at[step, h], up_s.at[step, h])

    def collect_done(step):
        @pl.when(self_out)
        def _():
            wait_recv(done.at[step, pl.ds(0, 6 * T)], ot_r.at[step])

        @pl.when(jnp.logical_not(self_out))
        def _():
            wait_recv(done.at[step], ot_r.at[step])

    def write(step):
        turned[step] = done[step].T
        pltpu.make_async_copy(turned.at[step], out.at[step], wr.at[step]).start()

    barrier = pltpu.get_barrier_semaphore()

    def greet(device):
        pl.semaphore_signal(barrier, inc=1, device_id=device, device_id_type=MESH)

    half = KNOWN // 2
    for part_of in range(2):
        groups = pl.ds(part_of * half, half)
        pltpu.make_async_copy(earlier.at[groups], y_raw.at[groups], ld.at[part_of]).start()
        pltpu.make_async_copy(factor.at[0, groups], f_raw.at[0, groups], ld.at[2 + part_of]).start()
    pltpu.make_async_copy(rhs, b_raw, ld.at[16]).start()

    def greet_plane(other):
        greet(at(x, (y + other // 4) % 4, (z + other % 4) % 4, j))

    for hop in range(4):
        for core in range(2):
            if (hop, core) != (0, 0):
                greet(at((x + hop) % 4, y, z, (j + core) % 2))
            greet(at((x + hop) % 4, y, (z + 1) % 4, (j + core) % 2))
            greet(at((x + hop) % 4, y, (z + 3) % 4, (j + core) % 2))
    loop(1, 16, greet_plane)
    load_inverse(0)
    load_update(PAIRS[0])
    load_known(1)

    def clear(tile):
        for step in range(STEPS):
            for h in range(CHAINS):
                res[step, h, tile] = jnp.zeros((T, 128), F32)

    loop(m + 1, 16, clear)

    def split_earlier(group):
        rows = pl.ds(pl.multiple_of(group * 128, 128), 128)
        high, low = halves(y_raw[group])
        y_parts[rows, 0:256] = high
        y_parts[rows, 256:512] = low

    both = None
    for part_of in range(2):
        groups = pl.ds(part_of * half, half)
        wait_local(y_raw.at[groups], ld.at[part_of])
        loop(part_of * half, (part_of + 1) * half, split_earlier)
        wait_local(f_raw.at[0, groups], ld.at[2 + part_of])
        split_known(0, part_of * half, (part_of + 1) * half)
        span = slice(part_of * half * 128, (part_of + 1) * half * 128)
        product = dot(f_parts[:, span], y_parts[span, :])
        both = product if both is None else both + product
    wait_local(b_raw, ld.at[16])
    finish_known(0, both)
    pl.semaphore_wait(barrier, 15 + 7 + 16)
    send_known(0)
    share_inverse(0)
    share_update(PAIRS[0])
    for step in range(2, STEPS):
        load_known(step)
    load_inverse(1)
    collect_known(0)
    for h in range(CHAINS):
        send_residual(0, h)
    prepare_inverse(0)
    for step in range(2, STEPS):
        load_inverse(step)
    for pair in PAIRS[1:]:
        load_update(pair)
    known_terms(1)
    send_known(1)
    prepare_update((1, 0))

    for step in range(STEPS):
        for h in range(CHAINS):
            solve(step, h)
        if step + 1 == STEPS:
            break
        for h in range(CHAINS):
            send_solution(step, h)
        for h in range(CHAINS):
            send_done(step, h)
        if step == 0:
            share_inverse(1)
            known_terms(2)
            send_known(2)
            collect_known(1)
            for pair in PAIRS[1:]:
                share_update(pair)
        elif step == 1:
            share_inverse(3)
            known_terms(3)
            send_known(3)
            collect_known(2)
            prepare_update((2, 1))
        elif step == 2:
            prepare_inverse(3)
            prepare_update((3, 2))
            collect_known(3)
        for h in range(CHAINS):
            gather_solution(step, h)
            update(step, step + 1, h)
        for h in range(CHAINS):
            send_residual(step + 1, h)
        if step == 0:
            prepare_inverse(1)
            share_inverse(2)
            prepare_update((2, 0))
            prepare_update((3, 0))
        elif step == 1:
            prepare_inverse(2)
            prepare_update((3, 1))
        for later_step in range(step + 2, STEPS):
            for h in range(CHAINS):
                update(step, later_step, h)
        collect_done(step)
        write(step)
        for h in range(CHAINS):
            drain_update(step, h)
            drain_residual(step, h)
            drain_part(step, h)
            drain_solution(step, h)

    for step in range(STEPS):
        wait_send(known.at[step, pl.ds(0, 192)], kn_s.at[step])
        wait_send(i_raw.at[step, j], sib_s.at[step])
    for slot in range(len(PAIRS)):
        wait_send(u_raw.at[slot, j], sib_s.at[4 + slot])
    for h in range(CHAINS):
        drain_residual(STEPS - 1, h)
    for h in range(CHAINS):
        collect_last(h)
    write(STEPS - 1)
    for h in range(CHAINS):
        drain_last(h)
    for step in range(STEPS):
        wait_local(turned.at[step], wr.at[step])


def per_device(factor, earlier, rhs, inverse):
    dma = pltpu.SemaphoreType.DMA
    vmem = pltpu.VMEM
    updates = len(PAIRS)
    return pl.pallas_call(
        kernel,
        out_shape=jax.ShapeDtypeStruct(rhs.shape, F32),
        in_specs=[pl.BlockSpec(memory_space=pl.ANY)] * 4,
        out_specs=pl.BlockSpec(memory_space=pl.ANY),
        scratch_shapes=[
            vmem((KNOWN, 128, 256), F32),
            vmem((KNOWN * 128, 512), BF16),
            vmem((STEPS, KNOWN, 128, 128), F32),
            vmem((256, KNOWN * 128), BF16),
            vmem((updates, 2, GROUPS, 128, 128), F32),
            vmem((updates, GROUPS * 128, 512), BF16),
            vmem((STEPS, 2, 16, 128, 128), F32),
            vmem((STEPS, 2048, 512), BF16),
            vmem((STEPS, 128, 256), F32),
            vmem((256, 128), F32),
            vmem((STEPS, 256, 128), F32),
            vmem((STEPS, 4, 64, 128), F32),
            vmem((STEPS, CHAINS, T, 128), F32),
            vmem((STEPS, CHAINS, 16, T, 128), F32),
            vmem((STEPS, CHAINS, 16, T, 128), F32),
            vmem((STEPS - 1, CHAINS, 4, T, 128), F32),
            vmem((STEPS, CHAINS, 2, T, 128), F32),
            vmem((STEPS, CHAINS, 2, T, 128), F32),
            vmem((STEPS - 1, CHAINS, 2, 2, T, 128), F32),
            vmem((2, CHAINS, 2, 2 * T, 128), F32),
            vmem((STEPS, 256, 128), F32),
            vmem((STEPS, 128, 256), F32),
            vmem((CHAINS, 4, 2, T, 128), F32),
            vmem((CHAINS, 2 * T, 2048), BF16),
            vmem((CHAINS, 4 * T, 1024), BF16),
            dma((20,)),
            dma((10,)),
            dma((10,)),
            dma((STEPS,)),
            dma((STEPS,)),
            dma((STEPS, CHAINS, 16)),
            dma((STEPS, CHAINS, 16)),
            dma((STEPS, CHAINS, 2)),
            dma((STEPS, CHAINS, 2)),
            dma((STEPS, CHAINS)),
            dma((STEPS, CHAINS)),
            dma((STEPS, CHAINS)),
            dma((STEPS,)),
            dma((STEPS, CHAINS)),
            dma((STEPS, CHAINS)),
            dma((CHAINS,)),
            dma((CHAINS,)),
            dma((STEPS,)),
        ],
        compiler_params=pltpu.CompilerParams(
            collective_id=0, has_side_effects=True, vmem_limit_bytes=60 * 1024 * 1024
        ),
        cost_estimate=pl.CostEstimate(flops=6_000_000_000, bytes_accessed=20_000_000, transcendentals=0),
        name="substitution",
    )(jnp.transpose(factor, (0, 2, 1, 3)), earlier, rhs, inverse)


def solution(mesh):
    return jax.shard_map(
        per_device,
        mesh=mesh,
        in_specs=(
            P(None, "row", None, "col"),
            P(None, "col", None),
            P(None, "row", None),
            P(None, "row", None),
        ),
        out_specs=P(None, "row", None),
        check_vma=False,
    )
```

```python
import functools

import jax
import jax.numpy as jnp
from jax import lax
from jax.experimental import pallas as pl
from jax.experimental.pallas import tpu as pltpu
from jax.sharding import PartitionSpec as P

F32 = jnp.float32
BF16 = jnp.bfloat16
MESH = pl.DeviceIdType.MESH
STEPS = 4
KNOWN = 20
GROUPS = 8
CHAINS = 2
T = 32
PLANE = [(2, 2), (2, 1), (2, 3), (1, 2), (3, 2), (2, 0), (0, 2), (1, 1), (1, 3), (3, 1), (3, 3), (1, 0), (3, 0), (0, 1), (0, 3)]
PAIRS = [(1, 0), (2, 0), (2, 1), (3, 0), (3, 1), (3, 2)]
SLOT = {pair: index for index, pair in enumerate(PAIRS)}


def halves(value):
    high = value.astype(BF16)
    return high, (value - high.astype(F32)).astype(BF16)


def dot(left, right):
    return lax.dot_general(left, right, (((1,), (0,)), ((), ())), preferred_element_type=F32)


def kernel(
    factor, earlier, rhs, inverse, out,
    y_raw, y_parts, f_raw, f_parts, u_raw, u_parts, i_raw, i_parts, b_raw, b_turn,
    known, known_in, start, res, sol, upd_in, part_in, part, upd, later, done, last_in, a_res, a_sol,
    ld, sib_s, sib_r, kn_s, kn_r, g1_s, g1_r, pt_s, pt_r, g2_s, g2_r, ot_s, ot_r, up_s, up_r, ls_s, ls_r,
):
    row = lax.axis_index("row")
    x = lax.axis_index("col")
    y, z, j = row // 8, (row // 2) % 4, row % 2
    m = row // 2

    def at(x_, y_, z_, j_):
        return ((y_ * 4 + z_) * 2 + j_, x_)

    sibling = at(x, y, z, 1 - j)
    own_zone = (z % 2) == (x // 2)
    g_here = jnp.where(own_zone, 0, 1)
    z_row = jnp.where(own_zone, z, (z + 3) % 4)
    q_here = (x + 2 * j + g_here) % 4
    sol_slot = g_here * 8 + y * 2 + z_row // 2
    self_part = own_zone & (j == 0)
    self_out = own_zone & (x % 2 == j)
    self_upd = j == 0

    def send(src, dst, ss, rs, device):
        pltpu.make_async_remote_copy(
            src_ref=src, dst_ref=dst, send_sem=ss, recv_sem=rs, device_id=device, device_id_type=MESH
        ).start()

    def wait_recv(ref, sem):
        pltpu.make_async_remote_copy(
            src_ref=ref, dst_ref=ref, send_sem=sem, recv_sem=sem, device_id=sibling, device_id_type=MESH
        ).wait_recv()

    def wait_send(ref, sem):
        pltpu.make_async_remote_copy(
            src_ref=ref, dst_ref=ref, send_sem=sem, recv_sem=sem, device_id=sibling, device_id_type=MESH
        ).wait_send()

    def wait_local(ref, sem):
        pltpu.make_async_copy(ref, ref, sem).wait()

    def loop(lo, hi, body):
        lax.fori_loop(lo, hi, lambda index, carry: (body(index), carry)[1], 0)

    def load_known(step):
        pltpu.make_async_copy(factor.at[step, pl.ds(0, KNOWN)], f_raw.at[step], ld.at[16 + step]).start()

    def load_inverse(step):
        def one(tile):
            lanes = pl.ds(pl.multiple_of((2 * tile + j) * 128, 128), 128)
            pltpu.make_async_copy(inverse.at[step, :, lanes], i_raw.at[step, j, tile], ld.at[6 + step]).start()

        loop(0, 16, one)

    def share_inverse(step):
        def one(tile):
            lanes = pl.ds(pl.multiple_of((2 * tile + 1 - j) * 128, 128), 128)
            send(inverse.at[step, :, lanes], i_raw.at[step, j, tile], sib_s.at[step], sib_r.at[step], sibling)

        loop(0, 16, one)

    def load_update(pair):
        later_step, step = pair
        slot = SLOT[pair]
        groups = pl.ds(KNOWN + step * GROUPS, GROUPS)
        pltpu.make_async_copy(factor.at[later_step, groups], u_raw.at[slot, j], ld.at[10 + slot]).start()

    def share_update(pair):
        slot = SLOT[pair]
        wait_local(u_raw.at[slot, j], ld.at[10 + slot])
        send(u_raw.at[slot, j], u_raw.at[slot, j], sib_s.at[4 + slot], sib_r.at[4 + slot], sibling)

    def prepare_inverse(step):
        wait_local(i_raw.at[step, j], ld.at[6 + step])
        wait_recv(i_raw.at[step, 1 - j], sib_r.at[step])

        def one(tile):
            rows = pl.ds(pl.multiple_of(tile * 128, 128), 128)
            for t in range(2):
                high, low = halves(i_raw[step, t, tile])
                i_parts[step, rows, t * 256 : t * 256 + 128] = high.T
                i_parts[step, rows, t * 256 + 128 : t * 256 + 256] = low.T

        loop(0, 16, one)

    def prepare_update(pair):
        slot = SLOT[pair]
        wait_recv(u_raw.at[slot, 1 - j], sib_r.at[4 + slot])

        def one(group):
            rows = pl.ds(pl.multiple_of(group * 128, 128), 128)
            for t in range(2):
                high, low = halves(u_raw[slot, t, group])
                u_parts[slot, rows, t * 256 : t * 256 + 128] = high.T
                u_parts[slot, rows, t * 256 + 128 : t * 256 + 256] = low.T

        loop(0, GROUPS, one)

    def split_known(step, first, end):
        def one(group):
            lanes = pl.ds(pl.multiple_of(group * 128, 128), 128)
            high, low = halves(f_raw[step, group])
            f_parts[0:128, lanes] = high
            f_parts[128:256, lanes] = low

        loop(first, end, one)

    def known_terms(step):
        wait_local(f_raw.at[step], ld.at[16 + step])
        split_known(step, 0, KNOWN)
        finish_known(step, dot(f_parts[...], y_parts[...]))

    def finish_known(step, both):
        total = both[0:128, 0:256] + (both[0:128, 256:512] + both[128:256, 0:256] + both[128:256, 256:512])
        known[step] = -(total.T)
        b_turn[...] = b_raw[step].T
        mine = pl.ds(pl.multiple_of(x * 64, 64), 64)
        known_in[step, x] = b_turn[mine] + known[step, mine]

    def send_known(step):
        for hop in (2, 1, 3):
            q = (x + hop) % 4
            rows = pl.ds(pl.multiple_of(q * 64, 64), 64)
            send(known.at[step, rows], known_in.at[step, x], kn_s.at[step], kn_r.at[step], at(q, y, z, j))

    def collect_known(step):
        wait_recv(known_in.at[step, pl.ds(0, 3)], kn_r.at[step])
        total = known_in[step, 0] + known_in[step, 1] + known_in[step, 2] + known_in[step, 3]
        for h in range(CHAINS):
            start[step, h] = total[h * T : (h + 1) * T]

    def send_residual(step, h):
        if step == 0:
            res[step, h, m] = start[step, h]
        else:

            @pl.when(self_upd)
            def _():
                wait_recv(upd_in.at[step - 1, h, pl.ds(0, 3)], up_r.at[step - 1, h])

            @pl.when(jnp.logical_not(self_upd))
            def _():
                wait_recv(upd_in.at[step - 1, h], up_r.at[step - 1, h])

            res[step, h, m] = start[step, h] + (
                upd_in[step - 1, h, 0] + upd_in[step - 1, h, 1] + upd_in[step - 1, h, 2] + upd_in[step - 1, h, 3]
            )

        def one(index):
            other = 16 + m - index
            send(
                res.at[step, h, m], res.at[step, h, m], g1_s.at[step, h, other], g1_r.at[step, h, m],
                at(x, other // 4, other % 4, j),
            )

        loop(m + 1, 16, one)

    def drain_residual(step, h):
        def one(other):
            wait_send(res.at[step, h, m], g1_s.at[step, h, other])

        loop(m + 1, 16, one)

    def solve(step, h):
        def arrived(tile):
            wait_recv(res.at[step, h, tile], g1_r.at[step, h, tile])

        loop(0, m, arrived)
        for tile in range(16):
            high, low = halves(res[step, h, tile])
            a_res[h, 0:T, tile * 128 : (tile + 1) * 128] = high
            a_res[h, T : 2 * T, tile * 128 : (tile + 1) * 128] = low
        both = dot(a_res[h], i_parts[step])
        for t in range(2):
            o = t * 256
            part[step, h, t] = both[0:T, o : o + 128] + (
                both[0:T, o + 128 : o + 256] + both[T : 2 * T, o : o + 128] + both[T : 2 * T, o + 128 : o + 256]
            )

        if step + 1 == STEPS:
            send_last(h)
            return

        def to(t):
            column = (z % 2) * 2 + t
            distance = (x + 4 - column) % 4
            send(
                part.at[step, h, t], part_in.at[step, h, j], pt_s.at[step, h, t], pt_r.at[step, h, j],
                at(column, y, (z + distance % 2) % 4, distance // 2),
            )

        for t in range(2):
            here = self_part & (x % 2 == t)

            @pl.when(here)
            def _():
                part_in[step, h, j] = part[step, h, t]

            @pl.when(jnp.logical_not(here))
            def _():
                to(t)

    def send_last(h):
        for t in range(2):
            for hop in (2, 1, 3):
                send(
                    part.at[STEPS - 1, h, t], last_in.at[h, x, j], ls_s.at[h], ls_r.at[h], at((x + hop) % 4, y, z, t)
                )
        last_in[h, x, j] = part[STEPS - 1, h, j]
        send(part.at[STEPS - 1, h, 1 - j], last_in.at[h, x, j], ls_s.at[h], ls_r.at[h], sibling)

    def collect_last(h):
        wait_recv(res.at[0, h, pl.ds(0, 7)], ls_r.at[h])
        for q in range(4):
            done[STEPS - 1, q * 64 + h * T : q * 64 + (h + 1) * T] = last_in[h, q, 0] + last_in[h, q, 1]

    def drain_last(h):
        wait_send(res.at[0, h, pl.ds(0, 7)], ls_s.at[h])

    def drain_part(step, h):
        for t in range(2):

            @pl.when(jnp.logical_not(self_part & (x % 2 == t)))
            def _():
                wait_send(part.at[step, h, t], pt_s.at[step, h, t])

    def send_solution(step, h):
        for k in range(2):

            @pl.when(jnp.logical_not(self_part & (j == k)))
            def _():
                wait_recv(part_in.at[step, h, k], pt_r.at[step, h, k])

        sol[step, h, sol_slot] = part_in[step, h, 0] + part_in[step, h, 1]
        mine = sol.at[step, h, sol_slot]
        for dy, dz in PLANE:
            send(mine, mine, g2_s.at[step, h], g2_r.at[step, h], at(x, (y + dy) % 4, (z + dz) % 4, j))

    def send_done(step, h):
        mine = sol.at[step, h, sol_slot]
        rows = pl.ds(pl.multiple_of(q_here * 64 + h * T, T), T)
        for hop in (2, 1, 3):
            send(mine, done.at[step, rows], ot_s.at[step, h], ot_r.at[step], at((x + hop) % 4, y, z_row, x % 2))

        @pl.when(self_out)
        def _():
            done[step, rows] = sol[step, h, sol_slot]

        @pl.when(jnp.logical_not(self_out))
        def _():
            send(mine, done.at[step, rows], ot_s.at[step, h], ot_r.at[step], at(x, y, z_row, x % 2))

    def drain_solution(step, h):
        wait_send(sol.at[step, h, pl.ds(0, 15)], g2_s.at[step, h])

        @pl.when(self_out)
        def _():
            wait_send(sol.at[step, h, pl.ds(0, 3)], ot_s.at[step, h])

        @pl.when(jnp.logical_not(self_out))
        def _():
            wait_send(sol.at[step, h, pl.ds(0, 4)], ot_s.at[step, h])

    def gather_solution(step, h):
        wait_recv(sol.at[step, h, pl.ds(0, 15)], g2_r.at[step, h])
        for g in range(2):
            for b in range(GROUPS):
                high, low = halves(sol[step, h, g * 8 + b])
                a_sol[h, g * T : (g + 1) * T, b * 128 : (b + 1) * 128] = high
                a_sol[h, 2 * T + g * T : 2 * T + (g + 1) * T, b * 128 : (b + 1) * 128] = low

    def update(step, later_step, h):
        both = dot(a_sol[h], u_parts[SLOT[later_step, step]])
        for t in range(2):
            o = t * 256
            total = both[0 : 2 * T, o : o + 128] + (
                both[0 : 2 * T, o + 128 : o + 256]
                + both[2 * T : 4 * T, o : o + 128]
                + both[2 * T : 4 * T, o + 128 : o + 256]
            )
            if step > 0:
                total = total + later[later_step - 2, h, t]
            if later_step > step + 1:
                later[later_step - 2, h, t] = total
            else:
                for g in range(2):
                    upd[step, h, t, g] = -total[g * T : (g + 1) * T]
        if later_step > step + 1:
            return
        for t in range(2):
            for g in range(2):
                here = (j == 0) & (g == 0) & (t == 0)

                @pl.when(here)
                def _():
                    upd_in[step, h, x] = upd[step, h, t, g]

                @pl.when(jnp.logical_not(here))
                def _():
                    send(
                        upd.at[step, h, t, g], upd_in.at[step, h, x], up_s.at[step, h], up_r.at[step, h],
                        at((x + 2 * j + g) % 4, y, z, t),
                    )

    def drain_update(step, h):
        @pl.when(self_upd)
        def _():
            wait_send(upd_in.at[step, h, pl.ds(0, 3)], up_s.at[step, h])

        @pl.when(jnp.logical_not(self_upd))
        def _():
            wait_send(upd_in.at[step, h], up_s.at[step, h])

    def collect_done(step):
        @pl.when(self_out)
        def _():
            wait_recv(done.at[step, pl.ds(0, 6 * T)], ot_r.at[step])

        @pl.when(jnp.logical_not(self_out))
        def _():
            wait_recv(done.at[step], ot_r.at[step])

    def write(step):
        out[step] = done[step].T

    barrier = pltpu.get_barrier_semaphore()

    def greet(device):
        pl.semaphore_signal(barrier, inc=1, device_id=device, device_id_type=MESH)

    half = KNOWN // 2
    for part_of in range(2):
        groups = pl.ds(part_of * half, half)
        pltpu.make_async_copy(earlier.at[groups], y_raw.at[groups], ld.at[part_of]).start()
        pltpu.make_async_copy(factor.at[0, groups], f_raw.at[0, groups], ld.at[2 + part_of]).start()
    pltpu.make_async_copy(rhs, b_raw, ld.at[16]).start()

    def greet_plane(other):
        greet(at(x, (y + other // 4) % 4, (z + other % 4) % 4, j))

    for hop in range(4):
        for core in range(2):
            if (hop, core) != (0, 0):
                greet(at((x + hop) % 4, y, z, (j + core) % 2))
            greet(at((x + hop) % 4, y, (z + 1) % 4, (j + core) % 2))
            greet(at((x + hop) % 4, y, (z + 3) % 4, (j + core) % 2))
    loop(1, 16, greet_plane)
    load_inverse(0)
    load_update(PAIRS[0])
    load_known(1)

    def clear(tile):
        for step in range(STEPS):
            for h in range(CHAINS):
                res[step, h, tile] = jnp.zeros((T, 128), F32)

    loop(m + 1, 16, clear)

    def split_earlier(group):
        rows = pl.ds(pl.multiple_of(group * 128, 128), 128)
        high, low = halves(y_raw[group])
        y_parts[rows, 0:256] = high
        y_parts[rows, 256:512] = low

    both = None
    for part_of in range(2):
        groups = pl.ds(part_of * half, half)
        wait_local(y_raw.at[groups], ld.at[part_of])
        loop(part_of * half, (part_of + 1) * half, split_earlier)
        wait_local(f_raw.at[0, groups], ld.at[2 + part_of])
        split_known(0, part_of * half, (part_of + 1) * half)
        span = slice(part_of * half * 128, (part_of + 1) * half * 128)
        product = dot(f_parts[:, span], y_parts[span, :])
        both = product if both is None else both + product
    wait_local(b_raw, ld.at[16])
    finish_known(0, both)
    pl.semaphore_wait(barrier, 15 + 7 + 16)
    send_known(0)
    share_inverse(0)
    share_update(PAIRS[0])
    for step in range(2, STEPS):
        load_known(step)
    load_inverse(1)
    collect_known(0)
    for h in range(CHAINS):
        send_residual(0, h)
    prepare_inverse(0)
    for step in range(2, STEPS):
        load_inverse(step)
    for pair in PAIRS[1:]:
        load_update(pair)
    known_terms(1)
    send_known(1)
    prepare_update((1, 0))

    for step in range(STEPS):
        for h in range(CHAINS):
            solve(step, h)
        if step + 1 == STEPS:
            break
        for h in range(CHAINS):
            send_solution(step, h)
        for h in range(CHAINS):
            send_done(step, h)
        if step == 0:
            share_inverse(1)
            known_terms(2)
            send_known(2)
            collect_known(1)
            for pair in PAIRS[1:]:
                share_update(pair)
        elif step == 1:
            share_inverse(3)
            known_terms(3)
            send_known(3)
            collect_known(2)
            prepare_update((2, 1))
        elif step == 2:
            prepare_inverse(3)
            prepare_update((3, 2))
            collect_known(3)
        for h in range(CHAINS):
            gather_solution(step, h)
            update(step, step + 1, h)
        for h in range(CHAINS):
            send_residual(step + 1, h)
        if step == 0:
            prepare_inverse(1)
            share_inverse(2)
            prepare_update((2, 0))
            prepare_update((3, 0))
        elif step == 1:
            prepare_inverse(2)
            prepare_update((3, 1))
        for later_step in range(step + 2, STEPS):
            for h in range(CHAINS):
                update(step, later_step, h)
        collect_done(step)
        write(step)
        for h in range(CHAINS):
            drain_update(step, h)
            drain_residual(step, h)
            drain_part(step, h)
            drain_solution(step, h)

    for step in range(STEPS):
        wait_send(known.at[step, pl.ds(0, 192)], kn_s.at[step])
        wait_send(i_raw.at[step, j], sib_s.at[step])
    for slot in range(len(PAIRS)):
        wait_send(u_raw.at[slot, j], sib_s.at[4 + slot])
    for h in range(CHAINS):
        drain_residual(STEPS - 1, h)
    for h in range(CHAINS):
        collect_last(h)
    write(STEPS - 1)
    for h in range(CHAINS):
        drain_last(h)


def per_device(factor, earlier, rhs, inverse):
    dma = pltpu.SemaphoreType.DMA
    vmem = pltpu.VMEM
    updates = len(PAIRS)
    return pl.pallas_call(
        kernel,
        out_shape=pltpu.VMEM(rhs.shape, F32),
        in_specs=[pl.BlockSpec(memory_space=pl.ANY)] * 4,
        out_specs=pl.BlockSpec(memory_space=pltpu.VMEM),
        scratch_shapes=[
            vmem((KNOWN, 128, 256), F32),
            vmem((KNOWN * 128, 512), BF16),
            vmem((STEPS, KNOWN, 128, 128), F32),
            vmem((256, KNOWN * 128), BF16),
            vmem((updates, 2, GROUPS, 128, 128), F32),
            vmem((updates, GROUPS * 128, 512), BF16),
            vmem((STEPS, 2, 16, 128, 128), F32),
            vmem((STEPS, 2048, 512), BF16),
            vmem((STEPS, 128, 256), F32),
            vmem((256, 128), F32),
            vmem((STEPS, 256, 128), F32),
            vmem((STEPS, 4, 64, 128), F32),
            vmem((STEPS, CHAINS, T, 128), F32),
            vmem((STEPS, CHAINS, 16, T, 128), F32),
            vmem((STEPS, CHAINS, 16, T, 128), F32),
            vmem((STEPS - 1, CHAINS, 4, T, 128), F32),
            vmem((STEPS, CHAINS, 2, T, 128), F32),
            vmem((STEPS, CHAINS, 2, T, 128), F32),
            vmem((STEPS - 1, CHAINS, 2, 2, T, 128), F32),
            vmem((2, CHAINS, 2, 2 * T, 128), F32),
            vmem((STEPS, 256, 128), F32),
            vmem((CHAINS, 4, 2, T, 128), F32),
            vmem((CHAINS, 2 * T, 2048), BF16),
            vmem((CHAINS, 4 * T, 1024), BF16),
            dma((20,)),
            dma((10,)),
            dma((10,)),
            dma((STEPS,)),
            dma((STEPS,)),
            dma((STEPS, CHAINS, 16)),
            dma((STEPS, CHAINS, 16)),
            dma((STEPS, CHAINS, 2)),
            dma((STEPS, CHAINS, 2)),
            dma((STEPS, CHAINS)),
            dma((STEPS, CHAINS)),
            dma((STEPS, CHAINS)),
            dma((STEPS,)),
            dma((STEPS, CHAINS)),
            dma((STEPS, CHAINS)),
            dma((CHAINS,)),
            dma((CHAINS,)),
        ],
        compiler_params=pltpu.CompilerParams(
            collective_id=0, has_side_effects=True, vmem_limit_bytes=60 * 1024 * 1024
        ),
        cost_estimate=pl.CostEstimate(flops=6_000_000_000, bytes_accessed=20_000_000, transcendentals=0),
        name="substitution",
    )(jnp.transpose(factor, (0, 2, 1, 3)), earlier, rhs, inverse)


def solution(mesh):
    return jax.shard_map(
        per_device,
        mesh=mesh,
        in_specs=(
            P(None, "row", None, "col"),
            P(None, "col", None),
            P(None, "row", None),
            P(None, "row", None),
        ),
        out_specs=P(None, "row", None),
        check_vma=False,
    )
```

```python
import functools

import jax
import jax.numpy as jnp
from jax import lax
from jax.experimental import pallas as pl
from jax.experimental.pallas import tpu as pltpu
from jax.sharding import PartitionSpec as P

F32 = jnp.float32
BF16 = jnp.bfloat16
MESH = pl.DeviceIdType.MESH
STEPS = 4
KNOWN = 20
GROUPS = 8
CHAINS = 2
T = 32
PLANE = [(2, 2), (2, 1), (2, 3), (1, 2), (3, 2), (2, 0), (0, 2), (1, 1), (1, 3), (3, 1), (3, 3), (1, 0), (3, 0), (0, 1), (0, 3)]
PAIRS = [(1, 0), (2, 0), (2, 1), (3, 0), (3, 1), (3, 2)]
SLOT = {pair: index for index, pair in enumerate(PAIRS)}


def halves(value):
    high = value.astype(BF16)
    return high, (value - high.astype(F32)).astype(BF16)


def dot(left, right):
    return lax.dot_general(left, right, (((1,), (0,)), ((), ())), preferred_element_type=F32)


def kernel(
    factor, earlier, rhs, inverse, out,
    y_raw, y_parts, f_raw, f_parts, u_raw, u_parts, i_raw, i_parts, b_raw, b_turn,
    known, known_in, start, res, sol, upd_in, part_in, part, upd, later, done, last_in, a_res, a_sol,
    ld, sib_s, sib_r, kn_s, kn_r, g1_s, g1_r, pt_s, pt_r, g2_s, g2_r, ot_s, ot_r, up_s, up_r, ls_s, ls_r,
):
    row = lax.axis_index("row")
    x = lax.axis_index("col")
    y, z, j = row // 8, (row // 2) % 4, row % 2
    m = row // 2

    def at(x_, y_, z_, j_):
        return ((y_ * 4 + z_) * 2 + j_, x_)

    sibling = at(x, y, z, 1 - j)
    own_zone = (z % 2) == (x // 2)
    g_here = jnp.where(own_zone, 0, 1)
    z_row = jnp.where(own_zone, z, (z + 3) % 4)
    q_here = (x + 2 * j + g_here) % 4
    sol_slot = g_here * 8 + y * 2 + z_row // 2
    self_part = own_zone & (j == 0)
    self_out = own_zone & (x % 2 == j)
    self_upd = j == 0

    def send(src, dst, ss, rs, device):
        pltpu.make_async_remote_copy(
            src_ref=src, dst_ref=dst, send_sem=ss, recv_sem=rs, device_id=device, device_id_type=MESH
        ).start()

    def wait_recv(ref, sem):
        pltpu.make_async_remote_copy(
            src_ref=ref, dst_ref=ref, send_sem=sem, recv_sem=sem, device_id=sibling, device_id_type=MESH
        ).wait_recv()

    def wait_send(ref, sem):
        pltpu.make_async_remote_copy(
            src_ref=ref, dst_ref=ref, send_sem=sem, recv_sem=sem, device_id=sibling, device_id_type=MESH
        ).wait_send()

    def wait_local(ref, sem):
        pltpu.make_async_copy(ref, ref, sem).wait()

    def loop(lo, hi, body):
        lax.fori_loop(lo, hi, lambda index, carry: (body(index), carry)[1], 0)

    def load_known(step):
        pltpu.make_async_copy(factor.at[step, pl.ds(0, KNOWN)], f_raw.at[step], ld.at[16 + step]).start()

    def load_inverse(step):
        def one(tile):
            lanes = pl.ds(pl.multiple_of((2 * tile + j) * 128, 128), 128)
            pltpu.make_async_copy(inverse.at[step, :, lanes], i_raw.at[step, j, tile], ld.at[6 + step]).start()

        loop(0, 16, one)

    def share_inverse(step):
        def one(tile):
            lanes = pl.ds(pl.multiple_of((2 * tile + 1 - j) * 128, 128), 128)
            send(inverse.at[step, :, lanes], i_raw.at[step, j, tile], sib_s.at[step], sib_r.at[step], sibling)

        loop(0, 16, one)

    def load_update(pair):
        later_step, step = pair
        slot = SLOT[pair]
        groups = pl.ds(KNOWN + step * GROUPS, GROUPS)
        pltpu.make_async_copy(factor.at[later_step, groups], u_raw.at[slot, j], ld.at[10 + slot]).start()

    def share_update(pair):
        slot = SLOT[pair]
        wait_local(u_raw.at[slot, j], ld.at[10 + slot])
        send(u_raw.at[slot, j], u_raw.at[slot, j], sib_s.at[4 + slot], sib_r.at[4 + slot], sibling)

    def prepare_inverse(step):
        wait_local(i_raw.at[step, j], ld.at[6 + step])
        wait_recv(i_raw.at[step, 1 - j], sib_r.at[step])

        def one(tile):
            rows = pl.ds(pl.multiple_of(tile * 128, 128), 128)
            for t in range(2):
                high, low = halves(i_raw[step, t, tile])
                i_parts[step, rows, t * 256 : t * 256 + 128] = high.T
                i_parts[step, rows, t * 256 + 128 : t * 256 + 256] = low.T

        loop(0, 16, one)

    def prepare_update(pair):
        slot = SLOT[pair]
        wait_recv(u_raw.at[slot, 1 - j], sib_r.at[4 + slot])

        def one(group):
            rows = pl.ds(pl.multiple_of(group * 128, 128), 128)
            for t in range(2):
                high, low = halves(u_raw[slot, t, group])
                u_parts[slot, rows, t * 256 : t * 256 + 128] = high.T
                u_parts[slot, rows, t * 256 + 128 : t * 256 + 256] = low.T

        loop(0, GROUPS, one)

    def split_known(step, first, end):
        def one(group):
            lanes = pl.ds(pl.multiple_of(group * 128, 128), 128)
            high, low = halves(f_raw[step, group])
            f_parts[0:128, lanes] = high
            f_parts[128:256, lanes] = low

        loop(first, end, one)

    def known_terms(step):
        wait_local(f_raw.at[step], ld.at[16 + step])
        split_known(step, 0, KNOWN)
        finish_known(step, dot(f_parts[...], y_parts[...]))

    def finish_known(step, both):
        total = both[0:128, 0:256] + (both[0:128, 256:512] + both[128:256, 0:256] + both[128:256, 256:512])
        known[step] = -(total.T)
        b_turn[...] = b_raw[step].T
        mine = pl.ds(pl.multiple_of(x * 64, 64), 64)
        known_in[step, x] = b_turn[mine] + known[step, mine]

    def send_known(step):
        for hop in (2, 1, 3):
            q = (x + hop) % 4
            rows = pl.ds(pl.multiple_of(q * 64, 64), 64)
            send(known.at[step, rows], known_in.at[step, x], kn_s.at[step], kn_r.at[step], at(q, y, z, j))

    def collect_known(step):
        wait_recv(known_in.at[step, pl.ds(0, 3)], kn_r.at[step])
        total = known_in[step, 0] + known_in[step, 1] + known_in[step, 2] + known_in[step, 3]
        for h in range(CHAINS):
            start[step, h] = total[h * T : (h + 1) * T]

    def send_residual(step, h):
        if step == 0:
            res[step, h, m] = start[step, h]
        else:

            @pl.when(self_upd)
            def _():
                wait_recv(upd_in.at[step - 1, h, pl.ds(0, 3)], up_r.at[step - 1, h])

            @pl.when(jnp.logical_not(self_upd))
            def _():
                wait_recv(upd_in.at[step - 1, h], up_r.at[step - 1, h])

            res[step, h, m] = start[step, h] + (
                upd_in[step - 1, h, 0] + upd_in[step - 1, h, 1] + upd_in[step - 1, h, 2] + upd_in[step - 1, h, 3]
            )

        def one(index):
            other = 16 + m - index
            y_to = other // 4
            send(
                res.at[step, h, m], res.at[step, h, m], g1_s.at[step, h, other],
                g1_r.at[step, h, jnp.where(y_to == y, 4 + z, y)], at(x, y_to, other % 4, j),
            )

        loop(m + 1, 16, one)

    def drain_residual(step, h):
        def one(other):
            wait_send(res.at[step, h, m], g1_s.at[step, h, other])

        loop(m + 1, 16, one)

    def solve(step, h):
        def arrived(other):
            wait_recv(res.at[step, h, y * 4 + other], g1_r.at[step, h, 4 + other])

        both = None
        for band in (3, 0, 2, 1):

            @pl.when(y == band)
            def _():
                loop(0, z, arrived)

            @pl.when(y > band)
            def _():
                wait_recv(res.at[step, h, pl.ds(band * 4, 4)], g1_r.at[step, h, band])

            for tile in range(band * 4, band * 4 + 4):
                high, low = halves(res[step, h, tile])
                a_res[h, 0:T, tile * 128 : (tile + 1) * 128] = high
                a_res[h, T : 2 * T, tile * 128 : (tile + 1) * 128] = low
            span = slice(band * 512, (band + 1) * 512)
            product = dot(a_res[h, :, span], i_parts[step, span, :])
            both = product if both is None else both + product
        for t in range(2):
            o = t * 256
            part[step, h, t] = both[0:T, o : o + 128] + (
                both[0:T, o + 128 : o + 256] + both[T : 2 * T, o : o + 128] + both[T : 2 * T, o + 128 : o + 256]
            )

        if step + 1 == STEPS:
            send_last(h)
            return

        def to(t):
            column = (z % 2) * 2 + t
            distance = (x + 4 - column) % 4
            send(
                part.at[step, h, t], part_in.at[step, h, j], pt_s.at[step, h, t], pt_r.at[step, h, j],
                at(column, y, (z + distance % 2) % 4, distance // 2),
            )

        for t in range(2):
            here = self_part & (x % 2 == t)

            @pl.when(here)
            def _():
                part_in[step, h, j] = part[step, h, t]

            @pl.when(jnp.logical_not(here))
            def _():
                to(t)

    def send_last(h):
        for t in range(2):
            for hop in (2, 1, 3):
                send(
                    part.at[STEPS - 1, h, t], last_in.at[h, x, j], ls_s.at[h], ls_r.at[h], at((x + hop) % 4, y, z, t)
                )
        last_in[h, x, j] = part[STEPS - 1, h, j]
        send(part.at[STEPS - 1, h, 1 - j], last_in.at[h, x, j], ls_s.at[h], ls_r.at[h], sibling)

    def collect_last(h):
        wait_recv(res.at[0, h, pl.ds(0, 7)], ls_r.at[h])
        for q in range(4):
            done[STEPS - 1, q * 64 + h * T : q * 64 + (h + 1) * T] = last_in[h, q, 0] + last_in[h, q, 1]

    def drain_last(h):
        wait_send(res.at[0, h, pl.ds(0, 7)], ls_s.at[h])

    def drain_part(step, h):
        for t in range(2):

            @pl.when(jnp.logical_not(self_part & (x % 2 == t)))
            def _():
                wait_send(part.at[step, h, t], pt_s.at[step, h, t])

    def send_solution(step, h):
        for k in range(2):

            @pl.when(jnp.logical_not(self_part & (j == k)))
            def _():
                wait_recv(part_in.at[step, h, k], pt_r.at[step, h, k])

        sol[step, h, sol_slot] = part_in[step, h, 0] + part_in[step, h, 1]
        mine = sol.at[step, h, sol_slot]
        for dy, dz in PLANE:
            send(mine, mine, g2_s.at[step, h], g2_r.at[step, h, dy], at(x, (y + dy) % 4, (z + dz) % 4, j))

    def send_done(step, h):
        mine = sol.at[step, h, sol_slot]
        rows = pl.ds(pl.multiple_of(q_here * 64 + h * T, T), T)
        for hop in (2, 1, 3):
            send(mine, done.at[step, rows], ot_s.at[step, h], ot_r.at[step], at((x + hop) % 4, y, z_row, x % 2))

        @pl.when(self_out)
        def _():
            done[step, rows] = sol[step, h, sol_slot]

        @pl.when(jnp.logical_not(self_out))
        def _():
            send(mine, done.at[step, rows], ot_s.at[step, h], ot_r.at[step], at(x, y, z_row, x % 2))

    def drain_solution(step, h):
        wait_send(sol.at[step, h, pl.ds(0, 15)], g2_s.at[step, h])

        @pl.when(self_out)
        def _():
            wait_send(sol.at[step, h, pl.ds(0, 3)], ot_s.at[step, h])

        @pl.when(jnp.logical_not(self_out))
        def _():
            wait_send(sol.at[step, h, pl.ds(0, 4)], ot_s.at[step, h])

    def gather_update(step, h):
        both = None
        for dy in (0, 1, 3, 2):
            wait_recv(sol.at[step, h, pl.ds(0, 4 if dy else 3)], g2_r.at[step, h, dy])
            source = (y + 4 - dy) % 4
            span = pl.ds(pl.multiple_of(source * 256, 256), 256)
            parts = []
            for g in range(2):
                parts.append([halves(sol[step, h, g * 8 + source * 2 + b]) for b in range(2)])
            left = jnp.concatenate(
                [jnp.concatenate([parts[g][b][side] for b in range(2)], axis=1) for side in range(2) for g in range(2)],
                axis=0,
            )
            a_sol[h, :, span] = left
            product = dot(left, u_parts[SLOT[step + 1, step], span, :])
            both = product if both is None else both + product
        finish_update(step, step + 1, h, both)

    def update(step, later_step, h):
        finish_update(step, later_step, h, dot(a_sol[h], u_parts[SLOT[later_step, step]]))

    def finish_update(step, later_step, h, both):
        for t in range(2):
            o = t * 256
            total = both[0 : 2 * T, o : o + 128] + (
                both[0 : 2 * T, o + 128 : o + 256]
                + both[2 * T : 4 * T, o : o + 128]
                + both[2 * T : 4 * T, o + 128 : o + 256]
            )
            if step > 0:
                total = total + later[later_step - 2, h, t]
            if later_step > step + 1:
                later[later_step - 2, h, t] = total
            else:
                for g in range(2):
                    upd[step, h, t, g] = -total[g * T : (g + 1) * T]
        if later_step > step + 1:
            return
        for t in range(2):
            for g in range(2):
                here = (j == 0) & (g == 0) & (t == 0)

                @pl.when(here)
                def _():
                    upd_in[step, h, x] = upd[step, h, t, g]

                @pl.when(jnp.logical_not(here))
                def _():
                    send(
                        upd.at[step, h, t, g], upd_in.at[step, h, x], up_s.at[step, h], up_r.at[step, h],
                        at((x + 2 * j + g) % 4, y, z, t),
                    )

    def drain_update(step, h):
        @pl.when(self_upd)
        def _():
            wait_send(upd_in.at[step, h, pl.ds(0, 3)], up_s.at[step, h])

        @pl.when(jnp.logical_not(self_upd))
        def _():
            wait_send(upd_in.at[step, h], up_s.at[step, h])

    def collect_done(step):
        @pl.when(self_out)
        def _():
            wait_recv(done.at[step, pl.ds(0, 6 * T)], ot_r.at[step])

        @pl.when(jnp.logical_not(self_out))
        def _():
            wait_recv(done.at[step], ot_r.at[step])

    def write(step):
        out[step] = done[step].T

    barrier = pltpu.get_barrier_semaphore()

    def greet(device):
        pl.semaphore_signal(barrier, inc=1, device_id=device, device_id_type=MESH)

    half = KNOWN // 2
    for part_of in range(2):
        groups = pl.ds(part_of * half, half)
        pltpu.make_async_copy(earlier.at[groups], y_raw.at[groups], ld.at[part_of]).start()
        pltpu.make_async_copy(factor.at[0, groups], f_raw.at[0, groups], ld.at[2 + part_of]).start()
    pltpu.make_async_copy(rhs, b_raw, ld.at[16]).start()

    def greet_plane(other):
        greet(at(x, (y + other // 4) % 4, (z + other % 4) % 4, j))

    for hop in range(4):
        for core in range(2):
            if (hop, core) != (0, 0):
                greet(at((x + hop) % 4, y, z, (j + core) % 2))
            greet(at((x + hop) % 4, y, (z + 1) % 4, (j + core) % 2))
            greet(at((x + hop) % 4, y, (z + 3) % 4, (j + core) % 2))
    loop(1, 16, greet_plane)
    load_inverse(0)
    load_update(PAIRS[0])
    load_known(1)

    def clear(tile):
        for step in range(STEPS):
            for h in range(CHAINS):
                res[step, h, tile] = jnp.zeros((T, 128), F32)

    loop(m + 1, 16, clear)

    def split_earlier(group):
        rows = pl.ds(pl.multiple_of(group * 128, 128), 128)
        high, low = halves(y_raw[group])
        y_parts[rows, 0:256] = high
        y_parts[rows, 256:512] = low

    both = None
    for part_of in range(2):
        groups = pl.ds(part_of * half, half)
        wait_local(y_raw.at[groups], ld.at[part_of])
        loop(part_of * half, (part_of + 1) * half, split_earlier)
        wait_local(f_raw.at[0, groups], ld.at[2 + part_of])
        split_known(0, part_of * half, (part_of + 1) * half)
        span = slice(part_of * half * 128, (part_of + 1) * half * 128)
        product = dot(f_parts[:, span], y_parts[span, :])
        both = product if both is None else both + product
    wait_local(b_raw, ld.at[16])
    finish_known(0, both)
    pl.semaphore_wait(barrier, 15 + 7 + 16)
    send_known(0)
    share_inverse(0)
    share_update(PAIRS[0])
    for step in range(2, STEPS):
        load_known(step)
    load_inverse(1)
    collect_known(0)
    for h in range(CHAINS):
        send_residual(0, h)
    prepare_inverse(0)
    for step in range(2, STEPS):
        load_inverse(step)
    for pair in PAIRS[1:]:
        load_update(pair)
    known_terms(1)
    send_known(1)
    prepare_update((1, 0))

    for step in range(STEPS):
        for h in range(CHAINS):
            solve(step, h)
        if step + 1 == STEPS:
            break
        for h in range(CHAINS):
            send_solution(step, h)
        for h in range(CHAINS):
            send_done(step, h)
        if step == 0:
            share_inverse(1)
            known_terms(2)
            send_known(2)
            collect_known(1)
            for pair in PAIRS[1:]:
                share_update(pair)
        elif step == 1:
            share_inverse(3)
            known_terms(3)
            send_known(3)
            collect_known(2)
            prepare_update((2, 1))
        elif step == 2:
            prepare_inverse(3)
            prepare_update((3, 2))
            collect_known(3)
        for h in range(CHAINS):
            gather_update(step, h)
        for h in range(CHAINS):
            send_residual(step + 1, h)
        if step == 0:
            prepare_inverse(1)
            share_inverse(2)
            prepare_update((2, 0))
            prepare_update((3, 0))
        elif step == 1:
            prepare_inverse(2)
            prepare_update((3, 1))
        for later_step in range(step + 2, STEPS):
            for h in range(CHAINS):
                update(step, later_step, h)
        collect_done(step)
        write(step)
        for h in range(CHAINS):
            drain_update(step, h)
            drain_residual(step, h)
            drain_part(step, h)
            drain_solution(step, h)

    for step in range(STEPS):
        wait_send(known.at[step, pl.ds(0, 192)], kn_s.at[step])
        wait_send(i_raw.at[step, j], sib_s.at[step])
    for slot in range(len(PAIRS)):
        wait_send(u_raw.at[slot, j], sib_s.at[4 + slot])
    for h in range(CHAINS):
        drain_residual(STEPS - 1, h)
    for h in range(CHAINS):
        collect_last(h)
    write(STEPS - 1)
    for h in range(CHAINS):
        drain_last(h)


def per_device(factor, earlier, rhs, inverse):
    dma = pltpu.SemaphoreType.DMA
    vmem = pltpu.VMEM
    updates = len(PAIRS)
    return pl.pallas_call(
        kernel,
        out_shape=pltpu.VMEM(rhs.shape, F32),
        in_specs=[pl.BlockSpec(memory_space=pl.ANY)] * 4,
        out_specs=pl.BlockSpec(memory_space=pltpu.VMEM),
        scratch_shapes=[
            vmem((KNOWN, 128, 256), F32),
            vmem((KNOWN * 128, 512), BF16),
            vmem((STEPS, KNOWN, 128, 128), F32),
            vmem((256, KNOWN * 128), BF16),
            vmem((updates, 2, GROUPS, 128, 128), F32),
            vmem((updates, GROUPS * 128, 512), BF16),
            vmem((STEPS, 2, 16, 128, 128), F32),
            vmem((STEPS, 2048, 512), BF16),
            vmem((STEPS, 128, 256), F32),
            vmem((256, 128), F32),
            vmem((STEPS, 256, 128), F32),
            vmem((STEPS, 4, 64, 128), F32),
            vmem((STEPS, CHAINS, T, 128), F32),
            vmem((STEPS, CHAINS, 16, T, 128), F32),
            vmem((STEPS, CHAINS, 16, T, 128), F32),
            vmem((STEPS - 1, CHAINS, 4, T, 128), F32),
            vmem((STEPS, CHAINS, 2, T, 128), F32),
            vmem((STEPS, CHAINS, 2, T, 128), F32),
            vmem((STEPS - 1, CHAINS, 2, 2, T, 128), F32),
            vmem((2, CHAINS, 2, 2 * T, 128), F32),
            vmem((STEPS, 256, 128), F32),
            vmem((CHAINS, 4, 2, T, 128), F32),
            vmem((CHAINS, 2 * T, 2048), BF16),
            vmem((CHAINS, 4 * T, 1024), BF16),
            dma((20,)),
            dma((10,)),
            dma((10,)),
            dma((STEPS,)),
            dma((STEPS,)),
            dma((STEPS, CHAINS, 16)),
            dma((STEPS, CHAINS, 8)),
            dma((STEPS, CHAINS, 2)),
            dma((STEPS, CHAINS, 2)),
            dma((STEPS, CHAINS)),
            dma((STEPS, CHAINS, 4)),
            dma((STEPS, CHAINS)),
            dma((STEPS,)),
            dma((STEPS, CHAINS)),
            dma((STEPS, CHAINS)),
            dma((CHAINS,)),
            dma((CHAINS,)),
        ],
        compiler_params=pltpu.CompilerParams(
            collective_id=0, has_side_effects=True, vmem_limit_bytes=60 * 1024 * 1024
        ),
        cost_estimate=pl.CostEstimate(flops=6_000_000_000, bytes_accessed=20_000_000, transcendentals=0),
        name="substitution",
    )(jnp.transpose(factor, (0, 2, 1, 3)), earlier, rhs, inverse)


def solution(mesh):
    return jax.shard_map(
        per_device,
        mesh=mesh,
        in_specs=(
            P(None, "row", None, "col"),
            P(None, "col", None),
            P(None, "row", None),
            P(None, "row", None),
        ),
        out_specs=P(None, "row", None),
        check_vma=False,
    )
```

```python
import functools

import jax
import jax.numpy as jnp
from jax import lax
from jax.experimental import pallas as pl
from jax.experimental.pallas import tpu as pltpu
from jax.sharding import PartitionSpec as P

F32 = jnp.float32
BF16 = jnp.bfloat16
MESH = pl.DeviceIdType.MESH
STEPS = 4
KNOWN = 20
GROUPS = 8
CHAINS = 2
T = 32
PLANE = [(2, 2), (2, 1), (2, 3), (1, 2), (3, 2), (2, 0), (0, 2), (1, 1), (1, 3), (3, 1), (3, 3), (1, 0), (3, 0), (0, 1), (0, 3)]
PAIRS = [(1, 0), (2, 0), (2, 1), (3, 0), (3, 1), (3, 2)]
SLOT = {pair: index for index, pair in enumerate(PAIRS)}


def halves(value):
    high = value.astype(BF16)
    return high, (value - high.astype(F32)).astype(BF16)


def dot(left, right):
    return lax.dot_general(left, right, (((1,), (0,)), ((), ())), preferred_element_type=F32)


def kernel(
    factor, earlier, rhs, inverse, out,
    y_raw, y_parts, f_raw, f_parts, u_raw, u_parts, i_raw, i_parts, b_raw, b_turn,
    known, known_in, start, res, sol, upd_in, part_in, part, upd, later, done, last_in, a_res, a_sol,
    ld, sib_s, sib_r, kn_s, kn_r, g1_s, g1_r, pt_s, pt_r, g2_s, g2_r, ot_s, ot_r, up_s, up_r, ls_s, ls_r,
):
    row = lax.axis_index("row")
    x = lax.axis_index("col")
    y, z, j = row // 8, (row // 2) % 4, row % 2
    m = row // 2

    def at(x_, y_, z_, j_):
        return ((y_ * 4 + z_) * 2 + j_, x_)

    sibling = at(x, y, z, 1 - j)
    own_zone = (z % 2) == (x // 2)
    g_here = jnp.where(own_zone, 0, 1)
    z_row = jnp.where(own_zone, z, (z + 3) % 4)
    q_here = (x + 2 * j + g_here) % 4
    sol_slot = g_here * 8 + y * 2 + z_row // 2
    self_part = own_zone & (j == 0)
    self_out = own_zone & (x % 2 == j)
    self_upd = j == 0

    def send(src, dst, ss, rs, device):
        pltpu.make_async_remote_copy(
            src_ref=src, dst_ref=dst, send_sem=ss, recv_sem=rs, device_id=device, device_id_type=MESH
        ).start()

    def wait_recv(ref, sem):
        pltpu.make_async_remote_copy(
            src_ref=ref, dst_ref=ref, send_sem=sem, recv_sem=sem, device_id=sibling, device_id_type=MESH
        ).wait_recv()

    def wait_send(ref, sem):
        pltpu.make_async_remote_copy(
            src_ref=ref, dst_ref=ref, send_sem=sem, recv_sem=sem, device_id=sibling, device_id_type=MESH
        ).wait_send()

    def wait_local(ref, sem):
        pltpu.make_async_copy(ref, ref, sem).wait()

    def loop(lo, hi, body):
        lax.fori_loop(lo, hi, lambda index, carry: (body(index), carry)[1], 0)

    def load_known(step):
        pltpu.make_async_copy(factor.at[step, pl.ds(0, KNOWN)], f_raw.at[step], ld.at[16 + step]).start()

    def load_inverse(step):
        def one(tile):
            lanes = pl.ds(pl.multiple_of((2 * tile + j) * 128, 128), 128)
            pltpu.make_async_copy(inverse.at[step, :, lanes], i_raw.at[step, j, tile], ld.at[6 + step]).start()

        loop(0, 16, one)

    def share_inverse(step):
        def one(tile):
            lanes = pl.ds(pl.multiple_of((2 * tile + 1 - j) * 128, 128), 128)
            send(inverse.at[step, :, lanes], i_raw.at[step, j, tile], sib_s.at[step], sib_r.at[step], sibling)

        loop(0, 16, one)

    def load_update(pair):
        later_step, step = pair
        slot = SLOT[pair]
        groups = pl.ds(KNOWN + step * GROUPS, GROUPS)
        pltpu.make_async_copy(factor.at[later_step, groups], u_raw.at[slot, j], ld.at[10 + slot]).start()

    def share_update(pair):
        slot = SLOT[pair]
        wait_local(u_raw.at[slot, j], ld.at[10 + slot])
        send(u_raw.at[slot, j], u_raw.at[slot, j], sib_s.at[4 + slot], sib_r.at[4 + slot], sibling)

    def prepare_inverse(step):
        wait_local(i_raw.at[step, j], ld.at[6 + step])
        wait_recv(i_raw.at[step, 1 - j], sib_r.at[step])

        def one(tile):
            rows = pl.ds(pl.multiple_of(tile * 128, 128), 128)
            for t in range(2):
                high, low = halves(i_raw[step, t, tile])
                i_parts[step, rows, t * 256 : t * 256 + 128] = high.T
                i_parts[step, rows, t * 256 + 128 : t * 256 + 256] = low.T

        loop(0, 16, one)

    def prepare_update(pair):
        slot = SLOT[pair]
        wait_recv(u_raw.at[slot, 1 - j], sib_r.at[4 + slot])

        def one(group):
            rows = pl.ds(pl.multiple_of(group * 128, 128), 128)
            for t in range(2):
                high, low = halves(u_raw[slot, t, group])
                u_parts[slot, rows, t * 256 : t * 256 + 128] = high.T
                u_parts[slot, rows, t * 256 + 128 : t * 256 + 256] = low.T

        loop(0, GROUPS, one)

    def split_known(step, first, end):
        def one(group):
            lanes = pl.ds(pl.multiple_of(group * 128, 128), 128)
            high, low = halves(f_raw[step, group])
            f_parts[0:128, lanes] = high
            f_parts[128:256, lanes] = low

        loop(first, end, one)

    def known_terms(step):
        wait_local(f_raw.at[step], ld.at[16 + step])
        split_known(step, 0, KNOWN)
        finish_known(step, dot(f_parts[...], y_parts[...]))

    def finish_known(step, both):
        total = both[0:128, 0:256] + (both[0:128, 256:512] + both[128:256, 0:256] + both[128:256, 256:512])
        known[step] = -(total.T)
        b_turn[...] = b_raw[step].T
        mine = pl.ds(pl.multiple_of(x * 64, 64), 64)
        known_in[step, x] = b_turn[mine] + known[step, mine]

    def send_known(step):
        for hop in (2, 1, 3):
            q = (x + hop) % 4
            rows = pl.ds(pl.multiple_of(q * 64, 64), 64)
            send(known.at[step, rows], known_in.at[step, x], kn_s.at[step], kn_r.at[step], at(q, y, z, j))

    def collect_known(step):
        wait_recv(known_in.at[step, pl.ds(0, 3)], kn_r.at[step])
        total = known_in[step, 0] + known_in[step, 1] + known_in[step, 2] + known_in[step, 3]
        for h in range(CHAINS):
            start[step, h] = total[h * T : (h + 1) * T]

    def send_residual(step, h):
        if step == 0:
            res[step, h, m] = start[step, h]
        else:

            @pl.when(self_upd)
            def _():
                wait_recv(upd_in.at[step - 1, h, pl.ds(0, 3)], up_r.at[step - 1, h])

            @pl.when(jnp.logical_not(self_upd))
            def _():
                wait_recv(upd_in.at[step - 1, h], up_r.at[step - 1, h])

            res[step, h, m] = start[step, h] + (
                upd_in[step - 1, h, 0] + upd_in[step - 1, h, 1] + upd_in[step - 1, h, 2] + upd_in[step - 1, h, 3]
            )

        def one(y_to, z_to, sem):
            send(
                res.at[step, h, m], res.at[step, h, m], g1_s.at[step, h, y_to * 4 + z_to], g1_r.at[step, h, sem],
                at(x, y_to, z_to, j),
            )

        def row_of_chips(index):
            for dz in (2, 1, 3, 0):
                one(4 + y - index, (z + dz) % 4, y)

        loop(y + 1, 4, row_of_chips)
        loop(z + 1, 4, lambda index: one(y, 4 + z - index, 4 + z))

    def drain_residual(step, h):
        def one(other):
            wait_send(res.at[step, h, m], g1_s.at[step, h, other])

        loop(m + 1, 16, one)

    def solve(step, h):
        def arrived(other):
            wait_recv(res.at[step, h, y * 4 + other], g1_r.at[step, h, 4 + other])

        both = None
        for band in (3, 0, 2, 1):

            @pl.when(y == band)
            def _():
                loop(0, z, arrived)

            @pl.when(y > band)
            def _():
                wait_recv(res.at[step, h, pl.ds(band * 4, 4)], g1_r.at[step, h, band])

            for tile in range(band * 4, band * 4 + 4):
                high, low = halves(res[step, h, tile])
                a_res[h, 0:T, tile * 128 : (tile + 1) * 128] = high
                a_res[h, T : 2 * T, tile * 128 : (tile + 1) * 128] = low
            span = slice(band * 512, (band + 1) * 512)
            product = dot(a_res[h, :, span], i_parts[step, span, :])
            both = product if both is None else both + product
        for t in range(2):
            o = t * 256
            part[step, h, t] = both[0:T, o : o + 128] + (
                both[0:T, o + 128 : o + 256] + both[T : 2 * T, o : o + 128] + both[T : 2 * T, o + 128 : o + 256]
            )

        if step + 1 == STEPS:
            send_last(h)
            return

        def to(t):
            column = (z % 2) * 2 + t
            distance = (x + 4 - column) % 4
            send(
                part.at[step, h, t], part_in.at[step, h, j], pt_s.at[step, h, t], pt_r.at[step, h, j],
                at(column, y, (z + distance % 2) % 4, distance // 2),
            )

        for t in range(2):
            here = self_part & (x % 2 == t)

            @pl.when(here)
            def _():
                part_in[step, h, j] = part[step, h, t]

            @pl.when(jnp.logical_not(here))
            def _():
                to(t)

    def send_last(h):
        for t in range(2):
            for hop in (2, 1, 3):
                send(
                    part.at[STEPS - 1, h, t], last_in.at[h, x, j], ls_s.at[h], ls_r.at[h], at((x + hop) % 4, y, z, t)
                )
        last_in[h, x, j] = part[STEPS - 1, h, j]
        send(part.at[STEPS - 1, h, 1 - j], last_in.at[h, x, j], ls_s.at[h], ls_r.at[h], sibling)

    def collect_last(h):
        wait_recv(res.at[0, h, pl.ds(0, 7)], ls_r.at[h])
        for q in range(4):
            done[STEPS - 1, q * 64 + h * T : q * 64 + (h + 1) * T] = last_in[h, q, 0] + last_in[h, q, 1]

    def drain_last(h):
        wait_send(res.at[0, h, pl.ds(0, 7)], ls_s.at[h])

    def drain_part(step, h):
        for t in range(2):

            @pl.when(jnp.logical_not(self_part & (x % 2 == t)))
            def _():
                wait_send(part.at[step, h, t], pt_s.at[step, h, t])

    def send_solution(step, h):
        for k in range(2):

            @pl.when(jnp.logical_not(self_part & (j == k)))
            def _():
                wait_recv(part_in.at[step, h, k], pt_r.at[step, h, k])

        sol[step, h, sol_slot] = part_in[step, h, 0] + part_in[step, h, 1]
        mine = sol.at[step, h, sol_slot]
        for dy, dz in PLANE:
            send(mine, mine, g2_s.at[step, h], g2_r.at[step, h, dy], at(x, (y + dy) % 4, (z + dz) % 4, j))

    def send_done(step, h):
        mine = sol.at[step, h, sol_slot]
        rows = pl.ds(pl.multiple_of(q_here * 64 + h * T, T), T)
        for hop in (2, 1, 3):
            send(mine, done.at[step, rows], ot_s.at[step, h], ot_r.at[step], at((x + hop) % 4, y, z_row, x % 2))

        @pl.when(self_out)
        def _():
            done[step, rows] = sol[step, h, sol_slot]

        @pl.when(jnp.logical_not(self_out))
        def _():
            send(mine, done.at[step, rows], ot_s.at[step, h], ot_r.at[step], at(x, y, z_row, x % 2))

    def drain_solution(step, h):
        wait_send(sol.at[step, h, pl.ds(0, 15)], g2_s.at[step, h])

        @pl.when(self_out)
        def _():
            wait_send(sol.at[step, h, pl.ds(0, 3)], ot_s.at[step, h])

        @pl.when(jnp.logical_not(self_out))
        def _():
            wait_send(sol.at[step, h, pl.ds(0, 4)], ot_s.at[step, h])

    def gather_update(step, h):
        both = None
        for dy in (0, 1, 3, 2):
            wait_recv(sol.at[step, h, pl.ds(0, 4 if dy else 3)], g2_r.at[step, h, dy])
            source = (y + 4 - dy) % 4
            span = pl.ds(pl.multiple_of(source * 256, 256), 256)
            parts = []
            for g in range(2):
                parts.append([halves(sol[step, h, g * 8 + source * 2 + b]) for b in range(2)])
            left = jnp.concatenate(
                [jnp.concatenate([parts[g][b][side] for b in range(2)], axis=1) for side in range(2) for g in range(2)],
                axis=0,
            )
            a_sol[h, :, span] = left
            product = dot(left, u_parts[SLOT[step + 1, step], span, :])
            both = product if both is None else both + product
        finish_update(step, step + 1, h, both)

    def update(step, later_step, h):
        finish_update(step, later_step, h, dot(a_sol[h], u_parts[SLOT[later_step, step]]))

    def finish_update(step, later_step, h, both):
        for t in range(2):
            o = t * 256
            total = both[0 : 2 * T, o : o + 128] + (
                both[0 : 2 * T, o + 128 : o + 256]
                + both[2 * T : 4 * T, o : o + 128]
                + both[2 * T : 4 * T, o + 128 : o + 256]
            )
            if step > 0:
                total = total + later[later_step - 2, h, t]
            if later_step > step + 1:
                later[later_step - 2, h, t] = total
            else:
                for g in range(2):
                    upd[step, h, t, g] = -total[g * T : (g + 1) * T]
        if later_step > step + 1:
            return
        for t in range(2):
            for g in range(2):
                here = (j == 0) & (g == 0) & (t == 0)

                @pl.when(here)
                def _():
                    upd_in[step, h, x] = upd[step, h, t, g]

                @pl.when(jnp.logical_not(here))
                def _():
                    send(
                        upd.at[step, h, t, g], upd_in.at[step, h, x], up_s.at[step, h], up_r.at[step, h],
                        at((x + 2 * j + g) % 4, y, z, t),
                    )

    def drain_update(step, h):
        @pl.when(self_upd)
        def _():
            wait_send(upd_in.at[step, h, pl.ds(0, 3)], up_s.at[step, h])

        @pl.when(jnp.logical_not(self_upd))
        def _():
            wait_send(upd_in.at[step, h], up_s.at[step, h])

    def collect_done(step):
        @pl.when(self_out)
        def _():
            wait_recv(done.at[step, pl.ds(0, 6 * T)], ot_r.at[step])

        @pl.when(jnp.logical_not(self_out))
        def _():
            wait_recv(done.at[step], ot_r.at[step])

    def write(step):
        out[step] = done[step].T

    barrier = pltpu.get_barrier_semaphore()

    def greet(device):
        pl.semaphore_signal(barrier, inc=1, device_id=device, device_id_type=MESH)

    half = KNOWN // 2
    for part_of in range(2):
        groups = pl.ds(part_of * half, half)
        pltpu.make_async_copy(earlier.at[groups], y_raw.at[groups], ld.at[part_of]).start()
        pltpu.make_async_copy(factor.at[0, groups], f_raw.at[0, groups], ld.at[2 + part_of]).start()
    pltpu.make_async_copy(rhs, b_raw, ld.at[16]).start()

    def greet_plane(other):
        greet(at(x, (y + other // 4) % 4, (z + other % 4) % 4, j))

    for hop in range(4):
        for core in range(2):
            if (hop, core) != (0, 0):
                greet(at((x + hop) % 4, y, z, (j + core) % 2))
            greet(at((x + hop) % 4, y, (z + 1) % 4, (j + core) % 2))
            greet(at((x + hop) % 4, y, (z + 3) % 4, (j + core) % 2))
    loop(1, 16, greet_plane)
    load_inverse(0)
    load_update(PAIRS[0])
    load_known(1)

    def clear(tile):
        for step in range(STEPS):
            for h in range(CHAINS):
                res[step, h, tile] = jnp.zeros((T, 128), F32)

    loop(m + 1, 16, clear)

    def split_earlier(group):
        rows = pl.ds(pl.multiple_of(group * 128, 128), 128)
        high, low = halves(y_raw[group])
        y_parts[rows, 0:256] = high
        y_parts[rows, 256:512] = low

    both = None
    for part_of in range(2):
        groups = pl.ds(part_of * half, half)
        wait_local(y_raw.at[groups], ld.at[part_of])
        loop(part_of * half, (part_of + 1) * half, split_earlier)
        wait_local(f_raw.at[0, groups], ld.at[2 + part_of])
        split_known(0, part_of * half, (part_of + 1) * half)
        span = slice(part_of * half * 128, (part_of + 1) * half * 128)
        product = dot(f_parts[:, span], y_parts[span, :])
        both = product if both is None else both + product
    wait_local(b_raw, ld.at[16])
    finish_known(0, both)
    pl.semaphore_wait(barrier, 15 + 7 + 16)
    send_known(0)
    share_inverse(0)
    share_update(PAIRS[0])
    for step in range(2, STEPS):
        load_known(step)
    load_inverse(1)
    collect_known(0)
    for h in range(CHAINS):
        send_residual(0, h)
    prepare_inverse(0)
    for step in range(2, STEPS):
        load_inverse(step)
    for pair in PAIRS[1:]:
        load_update(pair)
    known_terms(1)
    send_known(1)
    prepare_update((1, 0))

    for step in range(STEPS):
        for h in range(CHAINS):
            solve(step, h)
        if step + 1 == STEPS:
            break
        for h in range(CHAINS):
            send_solution(step, h)
        for h in range(CHAINS):
            send_done(step, h)
        if step == 0:
            share_inverse(1)
            known_terms(2)
            send_known(2)
            collect_known(1)
            for pair in PAIRS[1:]:
                share_update(pair)
        elif step == 1:
            share_inverse(3)
            known_terms(3)
            send_known(3)
            collect_known(2)
            prepare_update((2, 1))
        elif step == 2:
            prepare_inverse(3)
            prepare_update((3, 2))
            collect_known(3)
        for h in range(CHAINS):
            gather_update(step, h)
        for h in range(CHAINS):
            send_residual(step + 1, h)
        if step == 0:
            prepare_inverse(1)
            share_inverse(2)
            prepare_update((2, 0))
            prepare_update((3, 0))
        elif step == 1:
            prepare_inverse(2)
            prepare_update((3, 1))
        for later_step in range(step + 2, STEPS):
            for h in range(CHAINS):
                update(step, later_step, h)
        collect_done(step)
        write(step)
        for h in range(CHAINS):
            drain_update(step, h)
            drain_residual(step, h)
            drain_part(step, h)
            drain_solution(step, h)

    for step in range(STEPS):
        wait_send(known.at[step, pl.ds(0, 192)], kn_s.at[step])
        wait_send(i_raw.at[step, j], sib_s.at[step])
    for slot in range(len(PAIRS)):
        wait_send(u_raw.at[slot, j], sib_s.at[4 + slot])
    for h in range(CHAINS):
        drain_residual(STEPS - 1, h)
    for h in range(CHAINS):
        collect_last(h)
    write(STEPS - 1)
    for h in range(CHAINS):
        drain_last(h)


def per_device(factor, earlier, rhs, inverse):
    dma = pltpu.SemaphoreType.DMA
    vmem = pltpu.VMEM
    updates = len(PAIRS)
    return pl.pallas_call(
        kernel,
        out_shape=pltpu.VMEM(rhs.shape, F32),
        in_specs=[pl.BlockSpec(memory_space=pl.ANY)] * 4,
        out_specs=pl.BlockSpec(memory_space=pltpu.VMEM),
        scratch_shapes=[
            vmem((KNOWN, 128, 256), F32),
            vmem((KNOWN * 128, 512), BF16),
            vmem((STEPS, KNOWN, 128, 128), F32),
            vmem((256, KNOWN * 128), BF16),
            vmem((updates, 2, GROUPS, 128, 128), F32),
            vmem((updates, GROUPS * 128, 512), BF16),
            vmem((STEPS, 2, 16, 128, 128), F32),
            vmem((STEPS, 2048, 512), BF16),
            vmem((STEPS, 128, 256), F32),
            vmem((256, 128), F32),
            vmem((STEPS, 256, 128), F32),
            vmem((STEPS, 4, 64, 128), F32),
            vmem((STEPS, CHAINS, T, 128), F32),
            vmem((STEPS, CHAINS, 16, T, 128), F32),
            vmem((STEPS, CHAINS, 16, T, 128), F32),
            vmem((STEPS - 1, CHAINS, 4, T, 128), F32),
            vmem((STEPS, CHAINS, 2, T, 128), F32),
            vmem((STEPS, CHAINS, 2, T, 128), F32),
            vmem((STEPS - 1, CHAINS, 2, 2, T, 128), F32),
            vmem((2, CHAINS, 2, 2 * T, 128), F32),
            vmem((STEPS, 256, 128), F32),
            vmem((CHAINS, 4, 2, T, 128), F32),
            vmem((CHAINS, 2 * T, 2048), BF16),
            vmem((CHAINS, 4 * T, 1024), BF16),
            dma((20,)),
            dma((10,)),
            dma((10,)),
            dma((STEPS,)),
            dma((STEPS,)),
            dma((STEPS, CHAINS, 16)),
            dma((STEPS, CHAINS, 8)),
            dma((STEPS, CHAINS, 2)),
            dma((STEPS, CHAINS, 2)),
            dma((STEPS, CHAINS)),
            dma((STEPS, CHAINS, 4)),
            dma((STEPS, CHAINS)),
            dma((STEPS,)),
            dma((STEPS, CHAINS)),
            dma((STEPS, CHAINS)),
            dma((CHAINS,)),
            dma((CHAINS,)),
        ],
        compiler_params=pltpu.CompilerParams(
            collective_id=0, has_side_effects=True, vmem_limit_bytes=60 * 1024 * 1024
        ),
        cost_estimate=pl.CostEstimate(flops=6_000_000_000, bytes_accessed=20_000_000, transcendentals=0),
        name="substitution",
    )(jnp.transpose(factor, (0, 2, 1, 3)), earlier, rhs, inverse)


def solution(mesh):
    return jax.shard_map(
        per_device,
        mesh=mesh,
        in_specs=(
            P(None, "row", None, "col"),
            P(None, "col", None),
            P(None, "row", None),
            P(None, "row", None),
        ),
        out_specs=P(None, "row", None),
        check_vma=False,
    )
```
